32 devices in a mesh: pair: 4 (over x, core), virt: 8 (over z, y).
Axes of the slice: x: 2, y: 2, z: 4, core: 2. Of those that a mesh axis runs over, the one named last changes fastest.
Arguments:
- amplitudes: bfloat16 [1024, 256], P(('pair', 'virt')), may hold values from -6 to 6
- integrals: bfloat16 [256, 16384], P('pair', 'virt'), may hold values from -0.375 to 0.375
- amp_mask: int32 [16, 4], P('pair'), may hold values from 0 to 1, as said below
- integral_mask: int32 [4, 256], P('pair', 'virt'), may hold values 0 or 1
Outputs:
- ladder: bfloat16 [1024, 16384], P('pair', 'virt')
The draws below stay inside these ranges and needn't reach their ends.
Inputs may be any that keep to these rules, and one draw needn't show every extreme that they name: `amp_mask`: 0 or 1. For every block of 4 consecutive ij tiles, the cd tiles that hold nonzeros lie within one cyclic window of cd tiles common to the block, whose length may differ from block to block.
All inputs are finite; a program needn't handle non-finite values. No bound on the sum of `integral_mask` on one device may be relied on, other than what follows from the above.
Results may differ from the reference program's by a relative error of at most 0.001.
Values may be sent and summed in bfloat16 or wider, within the bound.
A program may use at most 64 MiB of HBM per device.

```python
import jax
import jax.numpy as jnp
from jax import lax

TILE = 64
IJ_DEV = 256
NIJ = 1024
NCD = 256
NAB = 16384


def draw_amp_mask(key, part):
    tile_rows = NIJ // TILE
    tile_columns = NCD // TILE
    per_block = IJ_DEV // TILE
    block_count = tile_rows // per_block
    centre_key = jax.random.fold_in(key, 11)
    width_key = jax.random.fold_in(key, 23)
    keep_key = jax.random.fold_in(key, 37)
    centre = jax.random.randint(centre_key, (block_count,), 0, tile_columns)
    widths = jax.random.randint(width_key, (block_count,), max(1, tile_columns // 4), tile_columns + 1)
    keeper = jax.random.randint(keep_key, (tile_rows, tile_columns), 0, 4) > 0
    block_of = jnp.arange(tile_rows) // per_block
    distance = (jnp.arange(tile_columns)[None, :] - centre[block_of][:, None]) % tile_columns
    inside = distance < widths[block_of][:, None]
    return (inside & keeper).astype(jnp.int32)


def plant(values, own_key, smallest, largest):
    index_at = [jax.random.randint(jax.random.fold_in(own_key, axis), (), 0, length) for axis, length in enumerate(values.shape)]
    longest = values.shape.index(max(values.shape))
    beside = index_at[:longest] + [(index_at[longest] + 1) % values.shape[longest]] + index_at[longest + 1:]
    return values.at[tuple(index_at)].set(smallest).at[tuple(beside)].set(largest)


def block_scale(rng, extent, cuts, least, high):
    gain, own = 1.0, jax.random.fold_in(rng, 6)
    for axis_at, blocks in cuts:
        draws = jnp.exp(jax.random.uniform(jax.random.fold_in(own, axis_at), (blocks,), jnp.float32, least / len(cuts), high / len(cuts)))
        gain = gain * jnp.repeat(draws, extent[axis_at] // blocks).reshape([-1 if axis == axis_at else 1 for axis in range(len(extent))])
    return gain


def bell_draw(stream_key, dims, spread, limit, shards=(), held_as=jnp.bfloat16):
    gain = block_scale(stream_key, dims, shards, -0.22, 0.18) if shards else 1.0
    values = jax.random.normal(stream_key, dims, jnp.float32) * spread * gain
    return jnp.minimum(jnp.maximum(values, -limit), limit).astype(held_as)


def setup_inputs(seed: int = 0) -> dict:
    key_of = jax.random.split(jax.random.key(seed), 5)
    amplitudes = bell_draw(key_of[0], (NIJ, NCD), 1.0, 6.0, ((0, 32),))
    integrals = bell_draw(key_of[1], (NCD, NAB), NCD ** -0.5, 0.375, ((0, 4), (1, 8)))
    amp_mask = draw_amp_mask(jax.random.fold_in(key_of[4], 71), 0)
    integral_mask = plant((jax.random.randint(key_of[3], (NCD // TILE, NAB // TILE), 0, 4) < 3).astype(jnp.int32), jax.random.fold_in(key_of[3], 1), 0, 1)
    return dict(amplitudes=amplitudes, integrals=integrals, amp_mask=amp_mask, integral_mask=integral_mask)


def widened_mask(values, mask):
    tile_rows, tile_columns = mask.shape
    shaped = values.reshape(tile_rows, TILE, tile_columns, TILE)
    return (shaped * mask.astype(values.dtype)[:, None, :, None]).reshape(values.shape)


def reference(amplitudes, integrals, amp_mask, integral_mask):
    tmask = widened_mask(amplitudes, amp_mask)
    virtual_mask = widened_mask(integrals, integral_mask)
    blocks = tmask.reshape(NIJ // IJ_DEV, IJ_DEV, NCD)

    def one_block(block_row_list):
        return jnp.dot(block_row_list, virtual_mask, preferred_element_type=jnp.float32).astype(jnp.bfloat16)

    result = lax.map(one_block, blocks)
    return result.reshape(NIJ, NAB)
```

```python
import functools

import jax
import jax.numpy as jnp
from jax import lax
from jax.experimental import pallas as pl
from jax.experimental.pallas import tpu as pltpu
from jax.sharding import PartitionSpec as P

MESH = pl.DeviceIdType.MESH
CHUNK = 256
CORES = 2
F32 = jnp.float32
BF16 = jnp.bfloat16


def spread(tiles, length, axis):
    shape = (length, tiles) if axis == 0 else (tiles, length)
    place = lax.broadcasted_iota(jnp.int32, shape, axis)
    tile = lax.broadcasted_iota(jnp.int32, shape, 1 - axis)
    size = length // tiles
    inside = (place >= tile * size) & (place < (tile + 1) * size)
    return jnp.where(inside, 1.0, 0.0).astype(BF16)


def kernel(n_pair, n_virt, amp_hbm, int_hbm, amp_mask, int_mask, out,
           own, panel, amps, masked, local_sem, x_send, x_recv, f_send, f_recv, a_send, a_recv):
    me_p, me_v = lax.axis_index("pair"), lax.axis_index("virt")
    n_hi = n_pair // CORES
    hi, core = me_p // CORES, me_p % CORES
    partner = hi * CORES + (1 - core)
    depth, columns = int_hbm.shape
    rows = amp_hbm.shape[0]
    chunks = panel.shape[0]

    load = pltpu.make_async_copy(int_hbm, own, local_sem.at[0])
    load.start()
    barrier = pltpu.get_barrier_semaphore()

    def hi_peer(step):
        return ((hi + step) % n_hi) * CORES + core

    def greet(pair, virt):
        pl.semaphore_signal(barrier, inc=1, device_id=(pair, virt), device_id_type=MESH)

    for step in range(1, n_virt):
        greet(me_p, (me_v + step) % n_virt)
    for step in range(1, n_hi):
        greet(hi_peer(step), me_v)
    greet(partner, me_v)

    my_amps = amps.at[pl.ds(pl.multiple_of(me_v * rows, rows), rows)]
    keep = pltpu.make_async_copy(amp_hbm, my_amps, local_sem.at[1])
    keep.start()

    def block(pair, chunk):
        return panel.at[chunk, pl.ds(pl.multiple_of(pair * depth, depth), depth)]

    tiles = int_mask.shape[1]
    mask = jnp.broadcast_to(int_mask[...].astype(F32), (8, tiles)).astype(BF16)
    wide = jnp.dot(mask, spread(tiles, columns, 1), preferred_element_type=F32)[:1].astype(BF16)
    load.wait()
    for c in range(chunks):
        at = slice(c * CHUNK, (c + 1) * CHUNK)
        block(me_p, c)[...] = own[:, at] * wide[:, at]

    pl.semaphore_wait(barrier, n_virt - 1 + n_hi)

    def to_hi(step, c):
        mine = block(me_p, c)
        return pltpu.make_async_remote_copy(
            src_ref=mine, dst_ref=mine, send_sem=x_send.at[step, c], recv_sem=x_recv.at[step, c],
            device_id=(hi_peer(step), me_v), device_id_type=MESH)

    def to_partner(step, c):
        held = block(((hi - step + n_hi) % n_hi) * CORES + core, c)
        return pltpu.make_async_remote_copy(
            src_ref=held, dst_ref=held, send_sem=f_send.at[step, c], recv_sem=f_recv.at[step, c],
            device_id=(partner, me_v), device_id_type=MESH)

    def to_virt(step):
        return pltpu.make_async_remote_copy(
            src_ref=amp_hbm, dst_ref=my_amps, send_sem=a_send.at[step], recv_sem=a_recv.at[step],
            device_id=(me_p, (me_v + step) % n_virt), device_id_type=MESH)

    for c in range(chunks):
        for step in range(1, n_hi):
            to_hi(step, c).start()
    for step in range(1, n_virt):
        to_virt(step).start()
    for c in range(chunks):
        to_partner(0, c).start()

    row_tiles, col_tiles = amp_mask.shape
    all_rows, depths = amps.shape
    tall = jnp.dot(spread(row_tiles, all_rows, 0), amp_mask[...].astype(F32).astype(BF16),
                   preferred_element_type=F32).astype(BF16)
    full = jnp.dot(tall, spread(col_tiles, depths, 1), preferred_element_type=F32).astype(BF16)
    keep.wait()
    for step in range(1, n_virt):
        to_virt(step).wait_recv()
    masked[...] = amps[...] * full

    def multiply(c):
        for step in range(n_hi):
            to_partner(step, c).wait_recv()
        part = min(all_rows, 256)

        def some_rows(r):
            at = pl.ds(r * part, part)
            total = jnp.dot(masked[at, :], panel[c], preferred_element_type=F32)
            out[at, c * CHUNK:(c + 1) * CHUNK] = total.astype(BF16)

        if all_rows == part:
            some_rows(0)
        else:
            def body(r, carry):
                some_rows(r)
                return carry
            lax.fori_loop(0, all_rows // part, body, 0)

    for c in range(chunks):
        for step in range(1, n_hi):
            to_hi(step, c).wait_recv()
            to_partner(step, c).start()
        if c:
            multiply(c - 1)
    multiply(chunks - 1)

    for step in range(1, n_virt):
        to_virt(step).wait_send()
    for c in range(chunks):
        for step in range(1, n_hi):
            to_hi(step, c).wait_send()
        for step in range(n_hi):
            to_partner(step, c).wait_send()


def solution(mesh):
    n_pair, n_virt = mesh.shape["pair"], mesh.shape["virt"]
    n_hi = n_pair // CORES

    def on_device(amplitudes, integrals, amp_mask, integral_mask):
        rows, depths = amplitudes.shape
        depth, columns = integrals.shape
        chunks = columns // CHUNK
        dma = pltpu.SemaphoreType.DMA
        vmem = pl.BlockSpec(memory_space=pltpu.VMEM)
        anywhere = pl.BlockSpec(memory_space=pl.ANY)
        return pl.pallas_call(
            functools.partial(kernel, n_pair, n_virt),
            out_shape=jax.ShapeDtypeStruct((rows * n_virt, columns), BF16),
            in_specs=[anywhere, anywhere, vmem, vmem],
            out_specs=vmem,
            scratch_shapes=[
                pltpu.VMEM((depth, columns), BF16),
                pltpu.VMEM((chunks, depths, CHUNK), BF16),
                pltpu.VMEM((rows * n_virt, depths), BF16),
                pltpu.VMEM((rows * n_virt, depths), BF16),
                dma((2,)),
                dma((n_hi, chunks)), dma((n_hi, chunks)),
                dma((n_hi, chunks)), dma((n_hi, chunks)),
                dma((n_virt,)), dma((n_virt,)),
            ],
            compiler_params=pltpu.CompilerParams(
                collective_id=0, has_side_effects=True, vmem_limit_bytes=32 * 2 ** 20),
        )(amplitudes, integrals, amp_mask, integral_mask)

    in_specs = (P(("pair", "virt"), None), P("pair", "virt"), P("pair", None), P("pair", "virt"))
    return jax.shard_map(
        on_device, mesh=mesh, in_specs=in_specs, out_specs=P("pair", "virt"), check_vma=False
    )
```

```python
import functools

import jax
import jax.numpy as jnp
from jax import lax
from jax.experimental import pallas as pl
from jax.experimental.pallas import tpu as pltpu
from jax.sharding import PartitionSpec as P

MESH = pl.DeviceIdType.MESH
CHUNK = 256
CORES = 2
F32 = jnp.float32
BF16 = jnp.bfloat16


def spread(tiles, length, axis):
    shape = (length, tiles) if axis == 0 else (tiles, length)
    place = lax.broadcasted_iota(jnp.int32, shape, axis)
    tile = lax.broadcasted_iota(jnp.int32, shape, 1 - axis)
    size = length // tiles
    inside = (place >= tile * size) & (place < (tile + 1) * size)
    return jnp.where(inside, 1.0, 0.0).astype(BF16)


def kernel(n_pair, n_virt, amp_hbm, int_hbm, amp_mask_hbm, int_mask_hbm, out,
           own, panel, amps, masked, amp_mask, int_mask, result,
           local_sem, out_sem, x_send, x_recv, f_send, f_recv, a_send, a_recv):
    me_p, me_v = lax.axis_index("pair"), lax.axis_index("virt")
    n_hi = n_pair // CORES
    hi, core = me_p // CORES, me_p % CORES
    partner = hi * CORES + (1 - core)
    depth, columns = int_hbm.shape
    rows = amp_hbm.shape[0]
    chunks = panel.shape[0]

    load = pltpu.make_async_copy(int_hbm, own, local_sem.at[0])
    load.start()
    load_int_mask = pltpu.make_async_copy(int_mask_hbm, int_mask, local_sem.at[2])
    load_int_mask.start()
    load_amp_mask = pltpu.make_async_copy(amp_mask_hbm, amp_mask, local_sem.at[3])
    load_amp_mask.start()
    barrier = pltpu.get_barrier_semaphore()

    def hi_peer(step):
        return ((hi + step) % n_hi) * CORES + core

    def greet(pair, virt):
        pl.semaphore_signal(barrier, inc=1, device_id=(pair, virt), device_id_type=MESH)

    for step in range(1, n_virt):
        greet(me_p, (me_v + step) % n_virt)
    for step in range(1, n_hi):
        greet(hi_peer(step), me_v)
    greet(partner, me_v)

    my_amps = amps.at[pl.ds(pl.multiple_of(me_v * rows, rows), rows)]
    keep = pltpu.make_async_copy(amp_hbm, my_amps, local_sem.at[1])
    keep.start()

    def block(pair, chunk):
        return panel.at[chunk, pl.ds(pl.multiple_of(pair * depth, depth), depth)]

    tiles = int_mask.shape[1]
    repeat = spread(tiles, columns, 1)
    load_int_mask.wait()
    mask = jnp.broadcast_to(int_mask[...].astype(F32), (8, tiles)).astype(BF16)
    wide = jnp.dot(mask, repeat, preferred_element_type=F32)[:1].astype(BF16)
    load.wait()
    for c in range(chunks):
        at = slice(c * CHUNK, (c + 1) * CHUNK)
        block(me_p, c)[...] = own[:, at] * wide[:, at]

    pl.semaphore_wait(barrier, n_virt - 1 + n_hi)

    def to_hi(step, c):
        mine = block(me_p, c)
        return pltpu.make_async_remote_copy(
            src_ref=mine, dst_ref=mine, send_sem=x_send.at[step, c], recv_sem=x_recv.at[step, c],
            device_id=(hi_peer(step), me_v), device_id_type=MESH)

    def to_partner(step, c):
        held = block(((hi - step + n_hi) % n_hi) * CORES + core, c)
        return pltpu.make_async_remote_copy(
            src_ref=held, dst_ref=held, send_sem=f_send.at[step, c], recv_sem=f_recv.at[step, c],
            device_id=(partner, me_v), device_id_type=MESH)

    def to_virt(step):
        return pltpu.make_async_remote_copy(
            src_ref=amp_hbm, dst_ref=my_amps, send_sem=a_send.at[step], recv_sem=a_recv.at[step],
            device_id=(me_p, (me_v + step) % n_virt), device_id_type=MESH)

    for step in range(1, n_virt):
        to_virt(step).start()
    for c in range(chunks):
        for step in range(1, n_hi):
            to_hi(step, c).start()
        to_partner(0, c).start()

    row_tiles, col_tiles = amp_mask.shape
    all_rows, depths = amps.shape
    load_amp_mask.wait()
    tall = jnp.dot(spread(row_tiles, all_rows, 0), amp_mask[...].astype(F32).astype(BF16),
                   preferred_element_type=F32).astype(BF16)
    masked[...] = jnp.dot(tall, spread(col_tiles, depths, 1), preferred_element_type=F32).astype(BF16)

    def gather_amps():
        keep.wait()
        for step in range(1, n_virt):
            to_virt(step).wait_recv()
        masked[...] = amps[...] * masked[...]

    def store(c):
        return pltpu.make_async_copy(result.at[c], out.at[:, pl.ds(c * CHUNK, CHUNK)], out_sem.at[c])

    def multiply(c):
        for step in range(n_hi):
            to_partner(step, c).wait_recv()
        part = min(all_rows, 256)

        def some_rows(r):
            at = pl.ds(r * part, part)
            total = jnp.dot(masked[at, :], panel[c], preferred_element_type=F32)
            result[c, at, :] = total.astype(BF16)

        if all_rows == part:
            some_rows(0)
        else:
            def body(r, carry):
                some_rows(r)
                return carry
            lax.fori_loop(0, all_rows // part, body, 0)
        store(c).start()

    late = chunks // 2
    for c in range(chunks):
        for step in range(1, n_hi):
            to_hi(step, c).wait_recv()
            to_partner(step, c).start()
        if c == late:
            gather_amps()
        if c >= late:
            for ready in range(0 if c == late else c - 1, c):
                multiply(ready)
    multiply(chunks - 1)

    for step in range(1, n_virt):
        to_virt(step).wait_send()
    for c in range(chunks):
        for step in range(1, n_hi):
            to_hi(step, c).wait_send()
        for step in range(n_hi):
            to_partner(step, c).wait_send()
        store(c).wait()


def solution(mesh):
    n_pair, n_virt = mesh.shape["pair"], mesh.shape["virt"]
    n_hi = n_pair // CORES

    def on_device(amplitudes, integrals, amp_mask, integral_mask):
        rows, depths = amplitudes.shape
        depth, columns = integrals.shape
        chunks = columns // CHUNK
        dma = pltpu.SemaphoreType.DMA
        hbm = pl.BlockSpec(memory_space=pltpu.HBM)
        return pl.pallas_call(
            functools.partial(kernel, n_pair, n_virt),
            out_shape=jax.ShapeDtypeStruct((rows * n_virt, columns), BF16),
            in_specs=[hbm] * 4,
            out_specs=hbm,
            scratch_shapes=[
                pltpu.VMEM((depth, columns), BF16),
                pltpu.VMEM((chunks, depths, CHUNK), BF16),
                pltpu.VMEM((rows * n_virt, depths), BF16),
                pltpu.VMEM((rows * n_virt, depths), BF16),
                pltpu.VMEM(amp_mask.shape, jnp.int32),
                pltpu.VMEM(integral_mask.shape, jnp.int32),
                pltpu.VMEM((chunks, rows * n_virt, CHUNK), BF16),
                dma((4,)),
                dma((chunks,)),
                dma((n_hi, chunks)), dma((n_hi, chunks)),
                dma((n_hi, chunks)), dma((n_hi, chunks)),
                dma((n_virt,)), dma((n_virt,)),
            ],
            compiler_params=pltpu.CompilerParams(
                collective_id=0, has_side_effects=True, vmem_limit_bytes=60 * 2 ** 20),
        )(amplitudes, integrals, amp_mask, integral_mask)

    in_specs = (P(("pair", "virt"), None), P("pair", "virt"), P("pair", None), P("pair", "virt"))
    return jax.shard_map(
        on_device, mesh=mesh, in_specs=in_specs, out_specs=P("pair", "virt"), check_vma=False
    )
```

```python
import functools

import jax
import jax.numpy as jnp
from jax import lax
from jax.experimental import pallas as pl
from jax.experimental.pallas import tpu as pltpu
from jax.sharding import PartitionSpec as P

MESH = pl.DeviceIdType.MESH
CHUNK = 256
CORES = 2
F32 = jnp.float32
BF16 = jnp.bfloat16


def spread(tiles, length, axis):
    shape = (length, tiles) if axis == 0 else (tiles, length)
    place = lax.broadcasted_iota(jnp.int32, shape, axis)
    tile = lax.broadcasted_iota(jnp.int32, shape, 1 - axis)
    size = length // tiles
    inside = (place >= tile * size) & (place < (tile + 1) * size)
    return jnp.where(inside, 1.0, 0.0).astype(BF16)


def kernel(n_pair, n_virt, amp_hbm, int_hbm, amp_mask_hbm, int_mask_hbm, out,
           own, panel, amps, masked, amp_mask, int_mask, result,
           local_sem, out_sem, x_send, x_recv, f_send, f_recv, a_send, a_recv):
    me_p, me_v = lax.axis_index("pair"), lax.axis_index("virt")
    n_hi = n_pair // CORES
    hi, core = me_p // CORES, me_p % CORES
    partner = hi * CORES + (1 - core)
    depth, columns = int_hbm.shape
    rows = amp_hbm.shape[0]
    chunks = panel.shape[0]

    load = pltpu.make_async_copy(int_hbm, own, local_sem.at[0])
    load.start()
    load_int_mask = pltpu.make_async_copy(int_mask_hbm, int_mask, local_sem.at[2])
    load_int_mask.start()
    load_amp_mask = pltpu.make_async_copy(amp_mask_hbm, amp_mask, local_sem.at[3])
    load_amp_mask.start()
    barrier = pltpu.get_barrier_semaphore()

    def hi_peer(step):
        return ((hi + step) % n_hi) * CORES + core

    rounds = n_virt.bit_length() - 1

    def virt_peer(turn):
        bit = 2 ** turn
        return me_v + bit * (1 - 2 * ((me_v // bit) % 2))

    def greet(pair, virt):
        pl.semaphore_signal(barrier, inc=1, device_id=(pair, virt), device_id_type=MESH)

    for turn in range(rounds):
        greet(me_p, virt_peer(turn))
    for step in range(1, n_hi):
        greet(hi_peer(step), me_v)
    greet(partner, me_v)

    my_amps = amps.at[pl.ds(pl.multiple_of(me_v * rows, rows), rows)]
    keep = pltpu.make_async_copy(amp_hbm, my_amps, local_sem.at[1])
    keep.start()

    def block(pair, chunk):
        return panel.at[chunk, pl.ds(pl.multiple_of(pair * depth, depth), depth)]

    tiles = int_mask.shape[1]
    repeat = spread(tiles, columns, 1)
    load_int_mask.wait()
    mask = jnp.broadcast_to(int_mask[...].astype(F32), (8, tiles)).astype(BF16)
    wide = jnp.dot(mask, repeat, preferred_element_type=F32)[:1].astype(BF16)
    load.wait()
    for c in range(chunks):
        at = slice(c * CHUNK, (c + 1) * CHUNK)
        block(me_p, c)[...] = own[:, at] * wide[:, at]

    pl.semaphore_wait(barrier, rounds + n_hi)

    def to_hi(step, c):
        mine = block(me_p, c)
        return pltpu.make_async_remote_copy(
            src_ref=mine, dst_ref=mine, send_sem=x_send.at[step, c], recv_sem=x_recv.at[step, c],
            device_id=(hi_peer(step), me_v), device_id_type=MESH)

    def to_partner(step, c):
        held = block(((hi - step + n_hi) % n_hi) * CORES + core, c)
        return pltpu.make_async_remote_copy(
            src_ref=held, dst_ref=held, send_sem=f_send.at[step, c], recv_sem=f_recv.at[step, c],
            device_id=(partner, me_v), device_id_type=MESH)

    def to_virt(turn):
        bit = 2 ** turn
        held = amps.at[pl.ds(pl.multiple_of((me_v // bit) * (bit * rows), bit * rows), bit * rows)]
        return pltpu.make_async_remote_copy(
            src_ref=held, dst_ref=held, send_sem=a_send.at[turn], recv_sem=a_recv.at[turn],
            device_id=(me_p, virt_peer(turn)), device_id_type=MESH)

    keep.wait()
    to_virt(0).start()
    for c in range(chunks):
        for step in range(1, n_hi):
            to_hi(step, c).start()
        to_partner(0, c).start()

    row_tiles, col_tiles = amp_mask.shape
    all_rows, depths = amps.shape
    load_amp_mask.wait()
    tall = jnp.dot(spread(row_tiles, all_rows, 0), amp_mask[...].astype(F32).astype(BF16),
                   preferred_element_type=F32).astype(BF16)
    masked[...] = jnp.dot(tall, spread(col_tiles, depths, 1), preferred_element_type=F32).astype(BF16)

    def store(c):
        return pltpu.make_async_copy(result.at[c], out.at[:, pl.ds(c * CHUNK, CHUNK)], out_sem.at[c])

    def multiply(c):
        for step in range(n_hi):
            to_partner(step, c).wait_recv()
        part = min(all_rows, 256)

        def some_rows(r):
            at = pl.ds(r * part, part)
            total = jnp.dot(masked[at, :], panel[c], preferred_element_type=F32)
            result[c, at, :] = total.astype(BF16)

        if all_rows == part:
            some_rows(0)
        else:
            def body(r, carry):
                some_rows(r)
                return carry
            lax.fori_loop(0, all_rows // part, body, 0)
        store(c).start()

    late = max(chunks // 2, rounds - 1)
    for c in range(chunks):
        if c + 1 < rounds:
            to_virt(c).wait_recv()
            to_virt(c + 1).start()
        for step in range(1, n_hi):
            to_hi(step, c).wait_recv()
            to_partner(step, c).start()
        if c == late:
            to_virt(rounds - 1).wait_recv()
            masked[...] = amps[...] * masked[...]
        if c >= late:
            for ready in range(0 if c == late else c - 1, c):
                multiply(ready)
    multiply(chunks - 1)

    for turn in range(rounds):
        to_virt(turn).wait_send()
    for c in range(chunks):
        for step in range(1, n_hi):
            to_hi(step, c).wait_send()
        for step in range(n_hi):
            to_partner(step, c).wait_send()
        store(c).wait()


def hand_over(held, out, sem):
    parts = sem.shape[0]
    size = held.shape[0] // parts
    copies = [pltpu.make_async_copy(held.at[pl.ds(i * size, size)], out.at[pl.ds(i * size, size)], sem.at[i])
              for i in range(parts)]
    for copy in copies:
        copy.start()
    for copy in copies:
        copy.wait()


def solution(mesh):
    n_pair, n_virt = mesh.shape["pair"], mesh.shape["virt"]
    n_hi = n_pair // CORES

    def on_device(amplitudes, integrals, amp_mask, integral_mask):
        rows, depths = amplitudes.shape
        depth, columns = integrals.shape
        chunks = columns // CHUNK
        dma = pltpu.SemaphoreType.DMA
        hbm = pl.BlockSpec(memory_space=pltpu.HBM)
        held = pl.pallas_call(
            functools.partial(kernel, n_pair, n_virt),
            out_shape=jax.ShapeDtypeStruct((rows * n_virt, columns), BF16),
            in_specs=[hbm] * 4,
            out_specs=hbm,
            scratch_shapes=[
                pltpu.VMEM((depth, columns), BF16),
                pltpu.VMEM((chunks, depths, CHUNK), BF16),
                pltpu.VMEM((rows * n_virt, depths), BF16),
                pltpu.VMEM((rows * n_virt, depths), BF16),
                pltpu.VMEM(amp_mask.shape, jnp.int32),
                pltpu.VMEM(integral_mask.shape, jnp.int32),
                pltpu.VMEM((chunks, rows * n_virt, CHUNK), BF16),
                dma((4,)),
                dma((chunks,)),
                dma((n_hi, chunks)), dma((n_hi, chunks)),
                dma((n_hi, chunks)), dma((n_hi, chunks)),
                dma((n_virt,)), dma((n_virt,)),
            ],
            compiler_params=pltpu.CompilerParams(
                collective_id=0, has_side_effects=True, vmem_limit_bytes=60 * 2 ** 20),
        )(amplitudes, integrals, amp_mask, integral_mask)
        return pl.pallas_call(
            hand_over,
            out_shape=jax.ShapeDtypeStruct(held.shape, held.dtype),
            in_specs=[hbm],
            out_specs=hbm,
            scratch_shapes=[dma((8,))],
            compiler_params=pltpu.CompilerParams(vmem_limit_bytes=60 * 2 ** 20),
        )(held)

    in_specs = (P(("pair", "virt"), None), P("pair", "virt"), P("pair", None), P("pair", "virt"))
    return jax.shard_map(
        on_device, mesh=mesh, in_specs=in_specs, out_specs=P("pair", "virt"), check_vma=False
    )
```

```python
import functools

import jax
import jax.numpy as jnp
from jax import lax
from jax.experimental import pallas as pl
from jax.experimental.pallas import tpu as pltpu
from jax.sharding import PartitionSpec as P

MESH = pl.DeviceIdType.MESH
CHUNK = 512
CORES = 2
F32 = jnp.float32
BF16 = jnp.bfloat16


def spread(tiles, length, axis):
    shape = (length, tiles) if axis == 0 else (tiles, length)
    place = lax.broadcasted_iota(jnp.int32, shape, axis)
    tile = lax.broadcasted_iota(jnp.int32, shape, 1 - axis)
    size = length // tiles
    inside = (place >= tile * size) & (place < (tile + 1) * size)
    return jnp.where(inside, 1.0, 0.0).astype(BF16)


def gather(n_pair, n_virt, amp_hbm, int_hbm, int_mask_hbm, panel, amps,
           own, own_amp, masked, landed, int_mask, load_sem, keep_sem, x_send, x_recv, x_keep,
           f_send, f_recv, a_send, a_recv):
    me_p, me_v = lax.axis_index("pair"), lax.axis_index("virt")
    n_hi = n_pair // CORES
    hi, core = me_p // CORES, me_p % CORES
    partner = hi * CORES + (1 - core)
    depth, columns = int_hbm.shape
    rows = amp_hbm.shape[0]
    chunks = panel.shape[0]

    loads = [pltpu.make_async_copy(src, dst, load_sem.at[i])
             for i, (src, dst) in enumerate(((int_mask_hbm, int_mask), (int_hbm, own), (amp_hbm, own_amp)))]
    for load in loads:
        load.start()
    barrier = pltpu.get_barrier_semaphore()

    def hi_peer(step):
        return ((hi + step) % n_hi) * CORES + core

    def greet(pair, virt):
        pl.semaphore_signal(barrier, inc=1, device_id=(pair, virt), device_id_type=MESH)

    for step in range(1, n_virt):
        greet(me_p, (me_v + step) % n_virt)
    for step in range(1, n_hi):
        greet(hi_peer(step), me_v)
    greet(partner, me_v)

    tiles = int_mask.shape[1]
    repeat = spread(tiles, columns, 1)
    loads[0].wait()
    mask = jnp.broadcast_to(int_mask[...].astype(F32), (8, tiles)).astype(BF16)
    wide = jnp.dot(mask, repeat, preferred_element_type=F32)[:1].astype(BF16)
    loads[1].wait()
    for c in range(chunks):
        at = slice(c * CHUNK, (c + 1) * CHUNK)
        masked[c] = own[:, at] * wide[:, at]
    loads[2].wait()

    pl.semaphore_wait(barrier, n_virt - 1 + n_hi)

    def rows_of(pair):
        return pl.ds(pl.multiple_of(pair * depth, depth), depth)

    my_amps = amps.at[pl.ds(pl.multiple_of(me_v * rows, rows), rows)]
    my_panel = panel.at[:, rows_of(me_p)]

    def to_hi(step, c):
        return pltpu.make_async_remote_copy(
            src_ref=masked.at[c], dst_ref=landed.at[step - 1, c],
            send_sem=x_send.at[step, c], recv_sem=x_recv.at[step, c],
            device_id=(hi_peer(step), me_v), device_id_type=MESH)

    def pass_on(step, c):
        held, place = landed.at[step - 1, c], panel.at[c, rows_of(((hi - step + n_hi) % n_hi) * CORES + core)]
        return pltpu.make_async_remote_copy(
            src_ref=held, dst_ref=place, send_sem=f_send.at[step, c], recv_sem=f_recv.at[step, c],
            device_id=(partner, me_v), device_id_type=MESH), pltpu.make_async_copy(held, place, x_keep.at[step, c])

    to_partner = pltpu.make_async_remote_copy(
        src_ref=masked, dst_ref=my_panel, send_sem=f_send.at[0, 0], recv_sem=f_recv.at[0, 0],
        device_id=(partner, me_v), device_id_type=MESH)

    def to_virt(step):
        return pltpu.make_async_remote_copy(
            src_ref=own_amp, dst_ref=my_amps, send_sem=a_send.at[step], recv_sem=a_recv.at[step],
            device_id=(me_p, (me_v + step) % n_virt), device_id_type=MESH)

    keeps = [pltpu.make_async_copy(masked, my_panel, keep_sem.at[0]),
             pltpu.make_async_copy(own_amp, my_amps, keep_sem.at[1])]
    for c in range(chunks):
        for step in range(1, n_hi):
            to_hi(step, c).start()
        if c == 0:
            for step in range(1, n_virt):
                to_virt(step).start()
    to_partner.start()
    for keep in keeps:
        keep.start()

    for c in range(chunks):
        for step in range(1, n_hi):
            to_hi(step, c).wait_recv()
            for copy in pass_on(step, c):
                copy.start()

    for keep in keeps:
        keep.wait()
    to_partner.wait()
    for step in range(1, n_virt):
        to_virt(step).wait()
    for c in range(chunks):
        for step in range(1, n_hi):
            to_hi(step, c).wait_send()
            for copy in pass_on(step, c):
                copy.wait()


def multiply(panel_hbm, amps_hbm, amp_mask_hbm, out, panel, amps, amp_mask, result, load_sem, panel_sem, out_sem):
    chunks = panel.shape[0]
    row_tiles, col_tiles = amp_mask.shape
    all_rows, depths = amps.shape
    part = min(all_rows, 256)
    loads = [pltpu.make_async_copy(amp_mask_hbm, amp_mask, load_sem.at[0]),
             pltpu.make_async_copy(amps_hbm, amps, load_sem.at[1])]
    blocks = [pltpu.make_async_copy(panel_hbm.at[c], panel.at[c], panel_sem.at[c]) for c in range(chunks)]
    stores = [pltpu.make_async_copy(result.at[c], out.at[:, pl.ds(c * CHUNK, CHUNK)], out_sem.at[c])
              for c in range(chunks)]
    for load in loads + blocks:
        load.start()
    tall, wide = spread(row_tiles, all_rows, 0), spread(col_tiles, depths, 1)
    loads[0].wait()
    tall = jnp.dot(tall, amp_mask[...].astype(F32).astype(BF16), preferred_element_type=F32).astype(BF16)
    full = jnp.dot(tall, wide, preferred_element_type=F32).astype(BF16)
    loads[1].wait()
    amps[...] = amps[...] * full

    for c in range(chunks):
        blocks[c].wait()

        def some_rows(r, carry):
            at = pl.ds(r * part, part)
            result[c, at, :] = jnp.dot(amps[at, :], panel[c], preferred_element_type=F32).astype(BF16)
            return carry

        if all_rows == part:
            some_rows(0, 0)
        else:
            lax.fori_loop(0, all_rows // part, some_rows, 0)
        stores[c].start()
    for store in stores:
        store.wait()


def solution(mesh):
    n_pair, n_virt = mesh.shape["pair"], mesh.shape["virt"]
    n_hi = n_pair // CORES

    def on_device(amplitudes, integrals, amp_mask, integral_mask):
        rows, depths = amplitudes.shape
        depth, columns = integrals.shape
        all_rows = rows * n_virt
        chunks = columns // CHUNK
        dma = pltpu.SemaphoreType.DMA
        hbm = pl.BlockSpec(memory_space=pltpu.HBM)
        whole_panel = jax.ShapeDtypeStruct((chunks, depths, CHUNK), BF16)
        whole_amps = jax.ShapeDtypeStruct((all_rows, depths), BF16)
        panel, amps = pl.pallas_call(
            functools.partial(gather, n_pair, n_virt),
            out_shape=(whole_panel, whole_amps),
            in_specs=[hbm] * 3,
            out_specs=(hbm, hbm),
            scratch_shapes=[
                pltpu.VMEM((depth, columns), BF16),
                pltpu.VMEM((rows, depths), BF16),
                pltpu.VMEM((chunks, depth, CHUNK), BF16),
                pltpu.VMEM((max(n_hi - 1, 1), chunks, depth, CHUNK), BF16),
                pltpu.VMEM(integral_mask.shape, jnp.int32),
                dma((3,)), dma((2,)),
                dma((n_hi, chunks)), dma((n_hi, chunks)), dma((n_hi, chunks)),
                dma((n_hi, chunks)), dma((n_hi, chunks)),
                dma((n_virt,)), dma((n_virt,)),
            ],
            compiler_params=pltpu.CompilerParams(
                collective_id=0, has_side_effects=True, vmem_limit_bytes=60 * 2 ** 20),
        )(amplitudes, integrals, integral_mask)
        return pl.pallas_call(
            multiply,
            out_shape=jax.ShapeDtypeStruct((all_rows, columns), BF16),
            in_specs=[hbm] * 3,
            out_specs=hbm,
            scratch_shapes=[
                pltpu.VMEM(whole_panel.shape, BF16),
                pltpu.VMEM(whole_amps.shape, BF16),
                pltpu.VMEM(amp_mask.shape, jnp.int32),
                pltpu.VMEM((chunks, all_rows, CHUNK), BF16),
                dma((2,)), dma((chunks,)), dma((chunks,)),
            ],
            compiler_params=pltpu.CompilerParams(vmem_limit_bytes=60 * 2 ** 20),
        )(panel, amps, amp_mask)

    in_specs = (P(("pair", "virt"), None), P("pair", "virt"), P("pair", None), P("pair", "virt"))
    return jax.shard_map(
        on_device, mesh=mesh, in_specs=in_specs, out_specs=P("pair", "virt"), check_vma=False
    )
```

```python
import functools

import jax
import jax.numpy as jnp
from jax import lax
from jax.experimental import pallas as pl
from jax.experimental.pallas import tpu as pltpu
from jax.sharding import PartitionSpec as P

MESH = pl.DeviceIdType.MESH
CHUNK = 256
FLIGHT = 3
CORES = 2
F32 = jnp.float32
BF16 = jnp.bfloat16


def spread(tiles, length, axis):
    shape = (length, tiles) if axis == 0 else (tiles, length)
    place = lax.broadcasted_iota(jnp.int32, shape, axis)
    tile = lax.broadcasted_iota(jnp.int32, shape, 1 - axis)
    size = length // tiles
    inside = (place >= tile * size) & (place < (tile + 1) * size)
    return jnp.where(inside, 1.0, 0.0).astype(BF16)


def gather(n_pair, n_virt, amp_hbm, int_hbm, amp_mask_hbm, int_mask_hbm, panel, amps_out,
           own, amps, masked, landed, amp_mask, int_mask, load_sem, keep_sem, x_send, x_recv, x_keep,
           f_send, f_recv, y_sem, up_send, up_recv, down_send, down_recv):
    me_p, me_v = lax.axis_index("pair"), lax.axis_index("virt")
    n_hi = n_pair // CORES
    hi, core = me_p // CORES, me_p % CORES
    partner = hi * CORES + (1 - core)
    depth, columns = int_hbm.shape
    rows = amp_hbm.shape[0]
    chunks = panel.shape[0]

    line, side = me_v // 2, me_v % 2
    n_line = n_virt // 2
    beside = line * 2 + (1 - side)
    my_amps = amps.at[pl.ds(pl.multiple_of(me_v * rows, rows), rows)]
    loads = [pltpu.make_async_copy(src, dst, load_sem.at[i])
             for i, (src, dst) in enumerate(((int_mask_hbm, int_mask), (int_hbm, own), (amp_hbm, my_amps),
                                             (amp_mask_hbm, amp_mask)))]
    for load in loads:
        load.start()
    barrier = pltpu.get_barrier_semaphore()

    def hi_peer(step):
        return ((hi + step) % n_hi) * CORES + core

    def greet(pair, virt):
        pl.semaphore_signal(barrier, inc=1, device_id=(pair, virt), device_id_type=MESH)

    greet(me_p, beside)
    pl.when(line > 0)(lambda: greet(me_p, me_v - 2))
    pl.when(line < n_line - 1)(lambda: greet(me_p, me_v + 2))
    for step in range(1, n_hi):
        greet(hi_peer(step), me_v)
    greet(partner, me_v)

    tiles = int_mask.shape[1]
    repeat = spread(tiles, columns, 1)
    loads[0].wait()
    mask = jnp.broadcast_to(int_mask[...].astype(F32), (8, tiles)).astype(BF16)
    wide = jnp.dot(mask, repeat, preferred_element_type=F32)[:1].astype(BF16)
    loads[1].wait()
    for c in range(chunks):
        at = slice(c * CHUNK, (c + 1) * CHUNK)
        masked[c] = own[:, at] * wide[:, at]
    loads[2].wait()

    below, above = (line + n_line - 1) // n_line, (2 * n_line - 2 - line) // n_line
    pl.semaphore_wait(barrier, n_hi + 1 + below + above)

    def rows_of(pair):
        return pl.ds(pl.multiple_of(pair * depth, depth), depth)

    my_panel = panel.at[:, rows_of(me_p)]

    def to_hi(step, c):
        return pltpu.make_async_remote_copy(
            src_ref=masked.at[c], dst_ref=landed.at[step - 1, c],
            send_sem=x_send.at[step, c], recv_sem=x_recv.at[step, c],
            device_id=(hi_peer(step), me_v), device_id_type=MESH)

    def pass_on(step, c):
        held, place = landed.at[step - 1, c], panel.at[c, rows_of(((hi - step + n_hi) % n_hi) * CORES + core)]
        return pltpu.make_async_remote_copy(
            src_ref=held, dst_ref=place, send_sem=f_send.at[step, c], recv_sem=f_recv.at[step, c],
            device_id=(partner, me_v), device_id_type=MESH), pltpu.make_async_copy(held, place, x_keep.at[step, c])

    to_partner = pltpu.make_async_remote_copy(
        src_ref=masked, dst_ref=my_panel, send_sem=f_send.at[0, 0], recv_sem=f_recv.at[0, 0],
        device_id=(partner, me_v), device_id_type=MESH)

    to_beside = pltpu.make_async_remote_copy(
        src_ref=my_amps, dst_ref=my_amps, send_sem=y_sem.at[0], recv_sem=y_sem.at[1],
        device_id=(me_p, beside), device_id_type=MESH)

    def two(place):
        return amps.at[pl.ds(pl.multiple_of(place * (2 * rows), 2 * rows), 2 * rows)]

    def up(step):
        held = two(line - step + 1)
        return pltpu.make_async_remote_copy(
            src_ref=held, dst_ref=held, send_sem=up_send.at[step], recv_sem=up_recv.at[step],
            device_id=(me_p, me_v + 2), device_id_type=MESH)

    def down(step):
        held = two(line + step - 1)
        return pltpu.make_async_remote_copy(
            src_ref=held, dst_ref=held, send_sem=down_send.at[step], recv_sem=down_recv.at[step],
            device_id=(me_p, me_v - 2), device_id_type=MESH)

    def up_goes(step):
        return (line < n_line - 1) & (line - step + 1 >= 0)

    def down_goes(step):
        return (line > 0) & (line + step - 1 < n_line)

    def line_start(step):
        pl.when(up_goes(step))(lambda: up(step).start())
        pl.when(down_goes(step))(lambda: down(step).start())

    def line_receive(step):
        pl.when(line - step >= 0)(lambda: up(step).wait_recv())
        pl.when(line + step < n_line)(lambda: down(step).wait_recv())

    def line_sent(step):
        pl.when(up_goes(step))(lambda: up(step).wait_send())
        pl.when(down_goes(step))(lambda: down(step).wait_send())

    def start_chunk(c):
        for step in range(1, n_hi):
            to_hi(step, c).start()

    keep = pltpu.make_async_copy(masked, my_panel, keep_sem.at[0])
    to_beside.start()
    for c in range(min(FLIGHT, chunks)):
        start_chunk(c)
    to_partner.start()
    keep.start()

    row_tiles, col_tiles = amp_mask.shape
    all_rows, depths = amps.shape
    loads[3].wait()
    tall = jnp.dot(spread(row_tiles, all_rows, 0), amp_mask[...].astype(F32).astype(BF16),
                   preferred_element_type=F32).astype(BF16)
    full = jnp.dot(tall, spread(col_tiles, depths, 1), preferred_element_type=F32).astype(BF16)

    to_beside.wait_recv()
    line_start(1)
    ahead = 1
    for c in range(chunks):
        for step in range(1, n_hi):
            to_hi(step, c).wait_send()
        if c + FLIGHT < chunks:
            start_chunk(c + FLIGHT)
        for step in range(1, n_hi):
            to_hi(step, c).wait_recv()
            for copy in pass_on(step, c):
                copy.start()
        if c % 2 == 1 and ahead < n_line - 1:
            line_receive(ahead)
            ahead += 1
            line_start(ahead)

    to_beside.wait_send()
    for step in range(ahead, n_line):
        line_receive(step)
        if step + 1 < n_line:
            line_start(step + 1)
    for step in range(1, n_line):
        line_sent(step)
    amps[...] = amps[...] * full
    amps_keep = pltpu.make_async_copy(amps, amps_out, keep_sem.at[1])
    amps_keep.start()

    keep.wait()
    to_partner.wait()
    for c in range(chunks):
        for step in range(1, n_hi):
            for copy in pass_on(step, c):
                copy.wait()
    amps_keep.wait()


def multiply(panel_hbm, amps_hbm, out, panel, amps, result, load_sem, panel_sem, out_sem):
    chunks = panel.shape[0]
    all_rows = amps.shape[0]
    part = min(all_rows, 256)
    load = pltpu.make_async_copy(amps_hbm, amps, load_sem.at[0])
    blocks = [pltpu.make_async_copy(panel_hbm.at[c], panel.at[c], panel_sem.at[c]) for c in range(chunks)]
    stores = [pltpu.make_async_copy(result.at[c], out.at[:, pl.ds(c * CHUNK, CHUNK)], out_sem.at[c])
              for c in range(chunks)]
    for copy in [load] + blocks:
        copy.start()
    load.wait()

    for c in range(chunks):
        blocks[c].wait()

        def some_rows(r, carry):
            at = pl.ds(r * part, part)
            result[c, at, :] = jnp.dot(amps[at, :], panel[c], preferred_element_type=F32).astype(BF16)
            return carry

        if all_rows == part:
            some_rows(0, 0)
        else:
            lax.fori_loop(0, all_rows // part, some_rows, 0)
        stores[c].start()
    for store in stores:
        store.wait()


def solution(mesh):
    n_pair, n_virt = mesh.shape["pair"], mesh.shape["virt"]
    n_hi = n_pair // CORES

    def on_device(amplitudes, integrals, amp_mask, integral_mask):
        rows, depths = amplitudes.shape
        depth, columns = integrals.shape
        all_rows = rows * n_virt
        chunks = columns // CHUNK
        dma = pltpu.SemaphoreType.DMA
        hbm = pl.BlockSpec(memory_space=pltpu.HBM)
        whole_panel = jax.ShapeDtypeStruct((chunks, depths, CHUNK), BF16)
        whole_amps = jax.ShapeDtypeStruct((all_rows, depths), BF16)
        panel, amps = pl.pallas_call(
            functools.partial(gather, n_pair, n_virt),
            out_shape=(whole_panel, whole_amps),
            in_specs=[hbm] * 4,
            out_specs=(hbm, hbm),
            scratch_shapes=[
                pltpu.VMEM((depth, columns), BF16),
                pltpu.VMEM((all_rows, depths), BF16),
                pltpu.VMEM((chunks, depth, CHUNK), BF16),
                pltpu.VMEM((max(n_hi - 1, 1), chunks, depth, CHUNK), BF16),
                pltpu.VMEM(amp_mask.shape, jnp.int32),
                pltpu.VMEM(integral_mask.shape, jnp.int32),
                dma((4,)), dma((2,)),
                dma((n_hi, chunks)), dma((n_hi, chunks)), dma((n_hi, chunks)),
                dma((n_hi, chunks)), dma((n_hi, chunks)),
                dma((2,)),
                dma((n_virt // 2,)), dma((n_virt // 2,)), dma((n_virt // 2,)), dma((n_virt // 2,)),
            ],
            compiler_params=pltpu.CompilerParams(
                collective_id=0, has_side_effects=True, vmem_limit_bytes=60 * 2 ** 20),
        )(amplitudes, integrals, amp_mask, integral_mask)
        return pl.pallas_call(
            multiply,
            out_shape=jax.ShapeDtypeStruct((all_rows, columns), BF16),
            in_specs=[hbm] * 2,
            out_specs=hbm,
            scratch_shapes=[
                pltpu.VMEM(whole_panel.shape, BF16),
                pltpu.VMEM(whole_amps.shape, BF16),
                pltpu.VMEM((chunks, all_rows, CHUNK), BF16),
                dma((1,)), dma((chunks,)), dma((chunks,)),
            ],
            compiler_params=pltpu.CompilerParams(vmem_limit_bytes=60 * 2 ** 20),
        )(panel, amps)

    in_specs = (P(("pair", "virt"), None), P("pair", "virt"), P("pair", None), P("pair", "virt"))
    return jax.shard_map(
        on_device, mesh=mesh, in_specs=in_specs, out_specs=P("pair", "virt"), check_vma=False
    )
```

```python
import functools

import jax
import jax.numpy as jnp
from jax import lax
from jax.experimental import pallas as pl
from jax.experimental.pallas import tpu as pltpu
from jax.sharding import PartitionSpec as P

MESH = pl.DeviceIdType.MESH
CHUNK = 1024
CORES = 2
F32 = jnp.float32
BF16 = jnp.bfloat16


def spread(tiles, length, axis):
    shape = (length, tiles) if axis == 0 else (tiles, length)
    place = lax.broadcasted_iota(jnp.int32, shape, axis)
    tile = lax.broadcasted_iota(jnp.int32, shape, 1 - axis)
    size = length // tiles
    inside = (place >= tile * size) & (place < (tile + 1) * size)
    return jnp.where(inside, 1.0, 0.0).astype(BF16)


def gather(n_pair, n_virt, amp_hbm, int_hbm, amp_mask_hbm, int_mask_hbm, panel, amps_out,
           own, amps, masked, landed, amp_mask, int_mask, load_sem, keep_sem, x_send, x_recv, x_keep,
           f_send, f_recv, a_send, a_recv):
    me_p, me_v = lax.axis_index("pair"), lax.axis_index("virt")
    n_hi = n_pair // CORES
    hi, core = me_p // CORES, me_p % CORES
    partner = hi * CORES + (1 - core)
    depth, columns = int_hbm.shape
    rows = amp_hbm.shape[0]
    chunks = panel.shape[0]

    my_amps = amps.at[pl.ds(pl.multiple_of(me_v * rows, rows), rows)]
    loads = [pltpu.make_async_copy(src, dst, load_sem.at[i])
             for i, (src, dst) in enumerate(((int_mask_hbm, int_mask), (int_hbm, own), (amp_hbm, my_amps),
                                             (amp_mask_hbm, amp_mask)))]
    for load in loads:
        load.start()
    barrier = pltpu.get_barrier_semaphore()

    def hi_peer(step):
        return ((hi + step) % n_hi) * CORES + core

    def greet(pair, virt):
        pl.semaphore_signal(barrier, inc=1, device_id=(pair, virt), device_id_type=MESH)

    for step in range(1, n_virt):
        greet(me_p, (me_v + step) % n_virt)
    for step in range(1, n_hi):
        greet(hi_peer(step), me_v)
    greet(partner, me_v)

    tiles = int_mask.shape[1]
    repeat = spread(tiles, columns, 1)
    loads[0].wait()
    mask = jnp.broadcast_to(int_mask[...].astype(F32), (8, tiles)).astype(BF16)
    wide = jnp.dot(mask, repeat, preferred_element_type=F32)[:1].astype(BF16)
    loads[1].wait()
    for c in range(chunks):
        at = slice(c * CHUNK, (c + 1) * CHUNK)
        masked[c] = own[:, at] * wide[:, at]
    loads[2].wait()

    pl.semaphore_wait(barrier, n_virt - 1 + n_hi)

    def rows_of(pair):
        return pl.ds(pl.multiple_of(pair * depth, depth), depth)

    my_panel = panel.at[:, rows_of(me_p)]

    def to_hi(step, c):
        return pltpu.make_async_remote_copy(
            src_ref=masked.at[c], dst_ref=landed.at[step - 1, c],
            send_sem=x_send.at[step, c], recv_sem=x_recv.at[step, c],
            device_id=(hi_peer(step), me_v), device_id_type=MESH)

    def pass_on(step, c):
        held, place = landed.at[step - 1, c], panel.at[c, rows_of(((hi - step + n_hi) % n_hi) * CORES + core)]
        return pltpu.make_async_remote_copy(
            src_ref=held, dst_ref=place, send_sem=f_send.at[step, c], recv_sem=f_recv.at[step, c],
            device_id=(partner, me_v), device_id_type=MESH), pltpu.make_async_copy(held, place, x_keep.at[step, c])

    to_partner = pltpu.make_async_remote_copy(
        src_ref=masked, dst_ref=my_panel, send_sem=f_send.at[0, 0], recv_sem=f_recv.at[0, 0],
        device_id=(partner, me_v), device_id_type=MESH)

    def to_virt(step):
        return pltpu.make_async_remote_copy(
            src_ref=my_amps, dst_ref=my_amps, send_sem=a_send.at[step], recv_sem=a_recv.at[step],
            device_id=(me_p, (me_v + step) % n_virt), device_id_type=MESH)

    keep = pltpu.make_async_copy(masked, my_panel, keep_sem.at[0])
    amps_keep = pltpu.make_async_copy(amps, amps_out, keep_sem.at[1])
    for c in range(chunks):
        for step in range(1, n_hi):
            to_hi(step, c).start()
        if c == 0:
            for step in range(1, n_virt):
                to_virt(step).start()
    to_partner.start()
    keep.start()

    row_tiles, col_tiles = amp_mask.shape
    all_rows, depths = amps.shape
    loads[3].wait()
    tall = jnp.dot(spread(row_tiles, all_rows, 0), amp_mask[...].astype(F32).astype(BF16),
                   preferred_element_type=F32).astype(BF16)
    full = jnp.dot(tall, spread(col_tiles, depths, 1), preferred_element_type=F32).astype(BF16)

    for c in range(chunks):
        if c == chunks - 1:
            for step in range(1, n_virt):
                to_virt(step).wait()
            amps[...] = amps[...] * full
            amps_keep.start()
        for step in range(1, n_hi):
            to_hi(step, c).wait_recv()
            for copy in pass_on(step, c):
                copy.start()

    keep.wait()
    to_partner.wait()
    amps_keep.wait()
    for c in range(chunks):
        for step in range(1, n_hi):
            to_hi(step, c).wait_send()
            for copy in pass_on(step, c):
                copy.wait()


def multiply(panel_hbm, amps_hbm, out, panel, amps, result, load_sem, panel_sem, out_sem):
    chunks = panel.shape[0]
    all_rows = amps.shape[0]
    part = min(all_rows, 256)
    load = pltpu.make_async_copy(amps_hbm, amps, load_sem.at[0])
    blocks = [pltpu.make_async_copy(panel_hbm.at[c], panel.at[c], panel_sem.at[c]) for c in range(chunks)]
    stores = [pltpu.make_async_copy(result.at[c], out.at[:, pl.ds(c * CHUNK, CHUNK)], out_sem.at[c])
              for c in range(chunks)]
    for copy in [load] + blocks:
        copy.start()
    load.wait()

    for c in range(chunks):
        blocks[c].wait()

        def some_rows(r, carry):
            at = pl.ds(r * part, part)
            result[c, at, :] = jnp.dot(amps[at, :], panel[c], preferred_element_type=F32).astype(BF16)
            return carry

        if all_rows == part:
            some_rows(0, 0)
        else:
            lax.fori_loop(0, all_rows // part, some_rows, 0)
        stores[c].start()
    for store in stores:
        store.wait()


def solution(mesh):
    n_pair, n_virt = mesh.shape["pair"], mesh.shape["virt"]
    n_hi = n_pair // CORES

    def on_device(amplitudes, integrals, amp_mask, integral_mask):
        rows, depths = amplitudes.shape
        depth, columns = integrals.shape
        all_rows = rows * n_virt
        chunks = columns // CHUNK
        dma = pltpu.SemaphoreType.DMA
        hbm = pl.BlockSpec(memory_space=pltpu.HBM)
        whole_panel = jax.ShapeDtypeStruct((chunks, depths, CHUNK), BF16)
        whole_amps = jax.ShapeDtypeStruct((all_rows, depths), BF16)
        panel, amps = pl.pallas_call(
            functools.partial(gather, n_pair, n_virt),
            out_shape=(whole_panel, whole_amps),
            in_specs=[hbm] * 4,
            out_specs=(hbm, hbm),
            scratch_shapes=[
                pltpu.VMEM((depth, columns), BF16),
                pltpu.VMEM((all_rows, depths), BF16),
                pltpu.VMEM((chunks, depth, CHUNK), BF16),
                pltpu.VMEM((max(n_hi - 1, 1), chunks, depth, CHUNK), BF16),
                pltpu.VMEM(amp_mask.shape, jnp.int32),
                pltpu.VMEM(integral_mask.shape, jnp.int32),
                dma((4,)), dma((2,)),
                dma((n_hi, chunks)), dma((n_hi, chunks)), dma((n_hi, chunks)),
                dma((n_hi, chunks)), dma((n_hi, chunks)),
                dma((n_virt,)), dma((n_virt,)),
            ],
            compiler_params=pltpu.CompilerParams(
                collective_id=0, has_side_effects=True, vmem_limit_bytes=60 * 2 ** 20),
        )(amplitudes, integrals, amp_mask, integral_mask)
        return pl.pallas_call(
            multiply,
            out_shape=jax.ShapeDtypeStruct((all_rows, columns), BF16),
            in_specs=[hbm] * 2,
            out_specs=hbm,
            scratch_shapes=[
                pltpu.VMEM(whole_panel.shape, BF16),
                pltpu.VMEM(whole_amps.shape, BF16),
                pltpu.VMEM((chunks, all_rows, CHUNK), BF16),
                dma((1,)), dma((chunks,)), dma((chunks,)),
            ],
            compiler_params=pltpu.CompilerParams(vmem_limit_bytes=60 * 2 ** 20),
        )(panel, amps)

    in_specs = (P(("pair", "virt"), None), P("pair", "virt"), P("pair", None), P("pair", "virt"))
    return jax.shard_map(
        on_device, mesh=mesh, in_specs=in_specs, out_specs=P("pair", "virt"), check_vma=False
    )
```

```python
import functools

import jax
import jax.numpy as jnp
from jax import lax
from jax.experimental import pallas as pl
from jax.experimental.pallas import tpu as pltpu
from jax.sharding import PartitionSpec as P

MESH = pl.DeviceIdType.MESH
CHUNK = 1024
CORES = 2
F32 = jnp.float32
BF16 = jnp.bfloat16


def spread(tiles, length, axis):
    shape = (length, tiles) if axis == 0 else (tiles, length)
    place = lax.broadcasted_iota(jnp.int32, shape, axis)
    tile = lax.broadcasted_iota(jnp.int32, shape, 1 - axis)
    size = length // tiles
    inside = (place >= tile * size) & (place < (tile + 1) * size)
    return jnp.where(inside, 1.0, 0.0).astype(BF16)


def gather(n_pair, n_virt, amp_hbm, int_hbm, amp_mask_hbm, int_mask_hbm, panel, amps_out,
           own, amps, masked, landed, amp_mask, int_mask, load_sem, keep_sem, x_send, x_recv, x_keep,
           f_send, f_recv, a_send, a_recv):
    me_p, me_v = lax.axis_index("pair"), lax.axis_index("virt")
    n_hi = n_pair // CORES
    hi, core = me_p // CORES, me_p % CORES
    partner = hi * CORES + (1 - core)
    depth, columns = int_hbm.shape
    rows = amp_hbm.shape[0]
    chunks = panel.shape[0]

    my_amps = amps.at[pl.ds(pl.multiple_of(me_v * rows, rows), rows)]
    loads = [pltpu.make_async_copy(src, dst, load_sem.at[i])
             for i, (src, dst) in enumerate(((int_mask_hbm, int_mask), (int_hbm, own), (amp_hbm, my_amps),
                                             (amp_mask_hbm, amp_mask)))]
    for load in loads:
        load.start()
    barrier = pltpu.get_barrier_semaphore()

    def hi_peer(step):
        return ((hi + step) % n_hi) * CORES + core

    def greet(pair, virt):
        pl.semaphore_signal(barrier, inc=1, device_id=(pair, virt), device_id_type=MESH)

    for step in range(1, n_virt):
        greet(me_p, (me_v + step) % n_virt)
    for step in range(1, n_hi):
        greet(hi_peer(step), me_v)
    greet(partner, me_v)

    tiles = int_mask.shape[1]
    repeat = spread(tiles, columns, 1)
    loads[0].wait()
    mask = jnp.broadcast_to(int_mask[...].astype(F32), (8, tiles)).astype(BF16)
    wide = jnp.dot(mask, repeat, preferred_element_type=F32)[:1].astype(BF16)
    loads[1].wait()
    for c in range(chunks):
        at = slice(c * CHUNK, (c + 1) * CHUNK)
        masked[c] = own[:, at] * wide[:, at]
    loads[2].wait()

    pl.semaphore_wait(barrier, n_virt - 1 + n_hi)

    def rows_of(pair):
        return pl.ds(pl.multiple_of(pair * depth, depth), depth)

    my_panel = panel.at[:, rows_of(me_p)]

    def to_hi(step, c):
        return pltpu.make_async_remote_copy(
            src_ref=masked.at[c], dst_ref=landed.at[step - 1, c],
            send_sem=x_send.at[step, c], recv_sem=x_recv.at[step, c],
            device_id=(hi_peer(step), me_v), device_id_type=MESH)

    def pass_on(step, c):
        held, place = landed.at[step - 1, c], panel.at[c, rows_of(((hi - step + n_hi) % n_hi) * CORES + core)]
        return pltpu.make_async_remote_copy(
            src_ref=held, dst_ref=place, send_sem=f_send.at[step, c], recv_sem=f_recv.at[step, c],
            device_id=(partner, me_v), device_id_type=MESH), pltpu.make_async_copy(held, place, x_keep.at[step, c])

    to_partner = pltpu.make_async_remote_copy(
        src_ref=masked, dst_ref=my_panel, send_sem=f_send.at[0, 0], recv_sem=f_recv.at[0, 0],
        device_id=(partner, me_v), device_id_type=MESH)

    def to_virt(step):
        return pltpu.make_async_remote_copy(
            src_ref=my_amps, dst_ref=my_amps, send_sem=a_send.at[step], recv_sem=a_recv.at[step],
            device_id=(me_p, (me_v + step) % n_virt), device_id_type=MESH)

    keep = pltpu.make_async_copy(masked, my_panel, keep_sem.at[0])
    amps_keep = pltpu.make_async_copy(amps, amps_out, keep_sem.at[1])
    def send_far():
        for c in range(chunks):
            for step in range(1, n_hi):
                to_hi(step, c).start()

    def send_rest():
        for step in range(1, n_virt):
            to_virt(step).start()
        to_partner.start()

    pl.when(core == 0)(send_far)
    send_rest()
    pl.when(core != 0)(send_far)
    keep.start()

    row_tiles, col_tiles = amp_mask.shape
    all_rows, depths = amps.shape
    loads[3].wait()
    tall = jnp.dot(spread(row_tiles, all_rows, 0), amp_mask[...].astype(F32).astype(BF16),
                   preferred_element_type=F32).astype(BF16)
    full = jnp.dot(tall, spread(col_tiles, depths, 1), preferred_element_type=F32).astype(BF16)

    for c in range(chunks):
        if c == chunks - 1:
            for step in range(1, n_virt):
                to_virt(step).wait()
            amps[...] = amps[...] * full
            amps_keep.start()
        for step in range(1, n_hi):
            to_hi(step, c).wait_recv()
            for copy in pass_on(step, c):
                copy.start()

    keep.wait()
    to_partner.wait()
    amps_keep.wait()
    for c in range(chunks):
        for step in range(1, n_hi):
            to_hi(step, c).wait_send()
            for copy in pass_on(step, c):
                copy.wait()


def multiply(panel_hbm, amps_hbm, out, panel, amps, result, load_sem, panel_sem, out_sem):
    chunks = panel.shape[0]
    all_rows = amps.shape[0]
    part = min(all_rows, 256)
    load = pltpu.make_async_copy(amps_hbm, amps, load_sem.at[0])
    blocks = [pltpu.make_async_copy(panel_hbm.at[c], panel.at[c], panel_sem.at[c]) for c in range(chunks)]
    stores = [pltpu.make_async_copy(result.at[c], out.at[:, pl.ds(c * CHUNK, CHUNK)], out_sem.at[c])
              for c in range(chunks)]
    for copy in [load] + blocks:
        copy.start()
    load.wait()

    for c in range(chunks):
        blocks[c].wait()

        def some_rows(r, carry):
            at = pl.ds(r * part, part)
            result[c, at, :] = jnp.dot(amps[at, :], panel[c], preferred_element_type=F32).astype(BF16)
            return carry

        if all_rows == part:
            some_rows(0, 0)
        else:
            lax.fori_loop(0, all_rows // part, some_rows, 0)
        stores[c].start()
    for store in stores:
        store.wait()


def solution(mesh):
    n_pair, n_virt = mesh.shape["pair"], mesh.shape["virt"]
    n_hi = n_pair // CORES

    def on_device(amplitudes, integrals, amp_mask, integral_mask):
        rows, depths = amplitudes.shape
        depth, columns = integrals.shape
        all_rows = rows * n_virt
        chunks = columns // CHUNK
        dma = pltpu.SemaphoreType.DMA
        hbm = pl.BlockSpec(memory_space=pltpu.HBM)
        whole_panel = jax.ShapeDtypeStruct((chunks, depths, CHUNK), BF16)
        whole_amps = jax.ShapeDtypeStruct((all_rows, depths), BF16)
        panel, amps = pl.pallas_call(
            functools.partial(gather, n_pair, n_virt),
            out_shape=(whole_panel, whole_amps),
            in_specs=[hbm] * 4,
            out_specs=(hbm, hbm),
            scratch_shapes=[
                pltpu.VMEM((depth, columns), BF16),
                pltpu.VMEM((all_rows, depths), BF16),
                pltpu.VMEM((chunks, depth, CHUNK), BF16),
                pltpu.VMEM((max(n_hi - 1, 1), chunks, depth, CHUNK), BF16),
                pltpu.VMEM(amp_mask.shape, jnp.int32),
                pltpu.VMEM(integral_mask.shape, jnp.int32),
                dma((4,)), dma((2,)),
                dma((n_hi, chunks)), dma((n_hi, chunks)), dma((n_hi, chunks)),
                dma((n_hi, chunks)), dma((n_hi, chunks)),
                dma((n_virt,)), dma((n_virt,)),
            ],
            compiler_params=pltpu.CompilerParams(
                collective_id=0, has_side_effects=True, vmem_limit_bytes=60 * 2 ** 20),
        )(amplitudes, integrals, amp_mask, integral_mask)
        return pl.pallas_call(
            multiply,
            out_shape=jax.ShapeDtypeStruct((all_rows, columns), BF16),
            in_specs=[hbm] * 2,
            out_specs=hbm,
            scratch_shapes=[
                pltpu.VMEM(whole_panel.shape, BF16),
                pltpu.VMEM(whole_amps.shape, BF16),
                pltpu.VMEM((chunks, all_rows, CHUNK), BF16),
                dma((1,)), dma((chunks,)), dma((chunks,)),
            ],
            compiler_params=pltpu.CompilerParams(vmem_limit_bytes=60 * 2 ** 20),
        )(panel, amps)

    in_specs = (P(("pair", "virt"), None), P("pair", "virt"), P("pair", None), P("pair", "virt"))
    return jax.shard_map(
        on_device, mesh=mesh, in_specs=in_specs, out_specs=P("pair", "virt"), check_vma=False
    )
```

```python
import functools

import jax
import jax.numpy as jnp
from jax import lax
from jax.experimental import pallas as pl
from jax.experimental.pallas import tpu as pltpu
from jax.sharding import PartitionSpec as P

MESH = pl.DeviceIdType.MESH
CHUNK = 1024
CORES = 2
F32 = jnp.float32
BF16 = jnp.bfloat16


def spread(tiles, length, axis):
    shape = (length, tiles) if axis == 0 else (tiles, length)
    place = lax.broadcasted_iota(jnp.int32, shape, axis)
    tile = lax.broadcasted_iota(jnp.int32, shape, 1 - axis)
    size = length // tiles
    inside = (place >= tile * size) & (place < (tile + 1) * size)
    return jnp.where(inside, 1.0, 0.0).astype(BF16)


def gather(n_pair, n_virt, amp_hbm, int_hbm, amp_mask_hbm, int_mask_hbm, panel, amps_out,
           own, amps, masked, landed, amp_mask, int_mask, load_sem, keep_sem, x_send, x_recv, x_keep,
           f_send, f_recv, a_send, a_recv, up_token, down_token):
    me_p, me_v = lax.axis_index("pair"), lax.axis_index("virt")
    n_hi = n_pair // CORES
    hi, core = me_p // CORES, me_p % CORES
    partner = hi * CORES + (1 - core)
    depth, columns = int_hbm.shape
    rows = amp_hbm.shape[0]
    chunks = panel.shape[0]

    line, side = me_v // 2, me_v % 2
    n_line = n_virt // 2
    my_amps = amps.at[pl.ds(pl.multiple_of(me_v * rows, rows), rows)]
    loads = [pltpu.make_async_copy(src, dst, load_sem.at[i])
             for i, (src, dst) in enumerate(((int_mask_hbm, int_mask), (int_hbm, own), (amp_hbm, my_amps),
                                             (amp_mask_hbm, amp_mask)))]
    for load in loads:
        load.start()
    barrier = pltpu.get_barrier_semaphore()

    def hi_peer(step):
        return ((hi + step) % n_hi) * CORES + core

    def greet(pair, virt):
        pl.semaphore_signal(barrier, inc=1, device_id=(pair, virt), device_id_type=MESH)

    greet(me_p, line * 2 + (1 - side))
    pl.when(line > 0)(lambda: greet(me_p, me_v - 2))
    pl.when(line < n_line - 1)(lambda: greet(me_p, me_v + 2))
    for step in range(1, n_hi):
        greet(hi_peer(step), me_v)
    greet(partner, me_v)

    tiles = int_mask.shape[1]
    repeat = spread(tiles, columns, 1)
    loads[0].wait()
    mask = jnp.broadcast_to(int_mask[...].astype(F32), (8, tiles)).astype(BF16)
    wide = jnp.dot(mask, repeat, preferred_element_type=F32)[:1].astype(BF16)
    loads[1].wait()
    for c in range(chunks):
        at = slice(c * CHUNK, (c + 1) * CHUNK)
        masked[c] = own[:, at] * wide[:, at]
    loads[2].wait()

    below, above = (line + n_line - 1) // n_line, (2 * n_line - 2 - line) // n_line
    pl.semaphore_wait(barrier, n_hi + 1 + below + above)

    def rows_of(pair):
        return pl.ds(pl.multiple_of(pair * depth, depth), depth)

    my_panel = panel.at[:, rows_of(me_p)]

    def to_hi(step, c):
        return pltpu.make_async_remote_copy(
            src_ref=masked.at[c], dst_ref=landed.at[step - 1, c],
            send_sem=x_send.at[step, c], recv_sem=x_recv.at[step, c],
            device_id=(hi_peer(step), me_v), device_id_type=MESH)

    def pass_on(step, c):
        held, place = landed.at[step - 1, c], panel.at[c, rows_of(((hi - step + n_hi) % n_hi) * CORES + core)]
        return pltpu.make_async_remote_copy(
            src_ref=held, dst_ref=place, send_sem=f_send.at[step, c], recv_sem=f_recv.at[step, c],
            device_id=(partner, me_v), device_id_type=MESH), pltpu.make_async_copy(held, place, x_keep.at[step, c])

    to_partner = pltpu.make_async_remote_copy(
        src_ref=masked, dst_ref=my_panel, send_sem=f_send.at[0, 0], recv_sem=f_recv.at[0, 0],
        device_id=(partner, me_v), device_id_type=MESH)

    def to_virt(step):
        other_side = side if step < n_line else 1 - side
        peer = ((line + step % n_line) % n_line) * 2 + other_side
        return pltpu.make_async_remote_copy(
            src_ref=my_amps, dst_ref=my_amps, send_sem=a_send.at[step], recv_sem=a_recv.at[step],
            device_id=(me_p, peer), device_id_type=MESH)

    def tell(token, step, virt):
        pl.semaphore_signal(token.at[step], inc=1, device_id=(me_p, virt), device_id_type=MESH)

    def tell_up(step):
        tell(up_token, step, me_v + 2)

    def tell_down(step):
        tell(down_token, step, me_v - 2)

    def reach(step):
        def below_side():
            pl.semaphore_wait(up_token.at[step], 1)
            if step + 1 < n_line:
                pl.when(line < n_line - 1)(lambda: tell_up(step + 1))
            to_virt(n_line - step).start()
            to_virt(2 * n_line - step).start()

        def above_side():
            pl.semaphore_wait(down_token.at[step], 1)
            if step + 1 < n_line:
                pl.when(line > 0)(lambda: tell_down(step + 1))
            to_virt(step).start()
            to_virt(n_line + step).start()

        pl.when(line - step >= 0)(below_side)
        pl.when(line + step < n_line)(above_side)

    keep = pltpu.make_async_copy(masked, my_panel, keep_sem.at[0])
    amps_keep = pltpu.make_async_copy(amps, amps_out, keep_sem.at[1])
    pl.when(line < n_line - 1)(lambda: tell_up(1))
    pl.when(line > 0)(lambda: tell_down(1))
    for step in range(1, n_hi):
        to_hi(step, 0).start()
    to_virt(n_line).start()
    for c in range(1, chunks):
        for step in range(1, n_hi):
            to_hi(step, c).start()
    to_partner.start()
    keep.start()
    for step in range(1, n_line):
        reach(step)

    row_tiles, col_tiles = amp_mask.shape
    all_rows, depths = amps.shape
    loads[3].wait()
    tall = jnp.dot(spread(row_tiles, all_rows, 0), amp_mask[...].astype(F32).astype(BF16),
                   preferred_element_type=F32).astype(BF16)
    full = jnp.dot(tall, spread(col_tiles, depths, 1), preferred_element_type=F32).astype(BF16)

    for c in range(chunks):
        for step in range(1, n_hi):
            to_hi(step, c).wait_recv()
            for copy in pass_on(step, c):
                copy.start()
    for step in range(1, n_virt):
        to_virt(step).wait()
    amps[...] = amps[...] * full
    amps_keep.start()

    keep.wait()
    to_partner.wait()
    amps_keep.wait()
    for c in range(chunks):
        for step in range(1, n_hi):
            to_hi(step, c).wait_send()
            for copy in pass_on(step, c):
                copy.wait()


def multiply(panel_hbm, amps_hbm, out, panel, amps, result, load_sem, panel_sem, out_sem):
    chunks = panel.shape[0]
    all_rows = amps.shape[0]
    part = min(all_rows, 256)
    load = pltpu.make_async_copy(amps_hbm, amps, load_sem.at[0])
    blocks = [pltpu.make_async_copy(panel_hbm.at[c], panel.at[c], panel_sem.at[c]) for c in range(chunks)]
    stores = [pltpu.make_async_copy(result.at[c], out.at[:, pl.ds(c * CHUNK, CHUNK)], out_sem.at[c])
              for c in range(chunks)]
    for copy in [load] + blocks:
        copy.start()
    load.wait()

    for c in range(chunks):
        blocks[c].wait()

        def some_rows(r, carry):
            at = pl.ds(r * part, part)
            result[c, at, :] = jnp.dot(amps[at, :], panel[c], preferred_element_type=F32).astype(BF16)
            return carry

        if all_rows == part:
            some_rows(0, 0)
        else:
            lax.fori_loop(0, all_rows // part, some_rows, 0)
        stores[c].start()
    for store in stores:
        store.wait()


def solution(mesh):
    n_pair, n_virt = mesh.shape["pair"], mesh.shape["virt"]
    n_hi = n_pair // CORES

    def on_device(amplitudes, integrals, amp_mask, integral_mask):
        rows, depths = amplitudes.shape
        depth, columns = integrals.shape
        all_rows = rows * n_virt
        chunks = columns // CHUNK
        dma = pltpu.SemaphoreType.DMA
        hbm = pl.BlockSpec(memory_space=pltpu.HBM)
        whole_panel = jax.ShapeDtypeStruct((chunks, depths, CHUNK), BF16)
        whole_amps = jax.ShapeDtypeStruct((all_rows, depths), BF16)
        panel, amps = pl.pallas_call(
            functools.partial(gather, n_pair, n_virt),
            out_shape=(whole_panel, whole_amps),
            in_specs=[hbm] * 4,
            out_specs=(hbm, hbm),
            scratch_shapes=[
                pltpu.VMEM((depth, columns), BF16),
                pltpu.VMEM((all_rows, depths), BF16),
                pltpu.VMEM((chunks, depth, CHUNK), BF16),
                pltpu.VMEM((max(n_hi - 1, 1), chunks, depth, CHUNK), BF16),
                pltpu.VMEM(amp_mask.shape, jnp.int32),
                pltpu.VMEM(integral_mask.shape, jnp.int32),
                dma((4,)), dma((2,)),
                dma((n_hi, chunks)), dma((n_hi, chunks)), dma((n_hi, chunks)),
                dma((n_hi, chunks)), dma((n_hi, chunks)),
                dma((n_virt,)), dma((n_virt,)),
                pltpu.SemaphoreType.REGULAR((n_virt // 2,)), pltpu.SemaphoreType.REGULAR((n_virt // 2,)),
            ],
            compiler_params=pltpu.CompilerParams(
                collective_id=0, has_side_effects=True, vmem_limit_bytes=60 * 2 ** 20),
        )(amplitudes, integrals, amp_mask, integral_mask)
        return pl.pallas_call(
            multiply,
            out_shape=jax.ShapeDtypeStruct((all_rows, columns), BF16),
            in_specs=[hbm] * 2,
            out_specs=hbm,
            scratch_shapes=[
                pltpu.VMEM(whole_panel.shape, BF16),
                pltpu.VMEM(whole_amps.shape, BF16),
                pltpu.VMEM((chunks, all_rows, CHUNK), BF16),
                dma((1,)), dma((chunks,)), dma((chunks,)),
            ],
            compiler_params=pltpu.CompilerParams(vmem_limit_bytes=60 * 2 ** 20),
        )(panel, amps)

    in_specs = (P(("pair", "virt"), None), P("pair", "virt"), P("pair", None), P("pair", "virt"))
    return jax.shard_map(
        on_device, mesh=mesh, in_specs=in_specs, out_specs=P("pair", "virt"), check_vma=False
    )
```

```python
import functools

import jax
import jax.numpy as jnp
from jax import lax
from jax.experimental import pallas as pl
from jax.experimental.pallas import tpu as pltpu
from jax.sharding import PartitionSpec as P

MESH = pl.DeviceIdType.MESH
CHUNK = 1024
CORES = 2
F32 = jnp.float32
BF16 = jnp.bfloat16


def spread(tiles, length, axis):
    shape = (length, tiles) if axis == 0 else (tiles, length)
    place = lax.broadcasted_iota(jnp.int32, shape, axis)
    tile = lax.broadcasted_iota(jnp.int32, shape, 1 - axis)
    size = length // tiles
    inside = (place >= tile * size) & (place < (tile + 1) * size)
    return jnp.where(inside, 1.0, 0.0).astype(BF16)


def gather(n_pair, n_virt, amp_hbm, int_hbm, amp_mask_hbm, int_mask_hbm, panel, amps, wide_out,
           own, own_amp, masked, landed, amp_mask, int_mask, wide_mask, load_sem, keep_sem, x_send, x_recv, x_keep,
           f_send, f_recv, a_send, a_recv, up_token, down_token):
    me_p, me_v = lax.axis_index("pair"), lax.axis_index("virt")
    n_hi = n_pair // CORES
    hi, core = me_p // CORES, me_p % CORES
    partner = hi * CORES + (1 - core)
    depth, columns = int_hbm.shape
    rows = amp_hbm.shape[0]
    chunks = panel.shape[0]

    line, side = me_v // 2, me_v % 2
    n_line = n_virt // 2
    my_amps = amps.at[pl.ds(pl.multiple_of(me_v * rows, rows), rows)]
    loads = [pltpu.make_async_copy(src, dst, load_sem.at[i])
             for i, (src, dst) in enumerate(((int_mask_hbm, int_mask), (int_hbm, own), (amp_hbm, own_amp),
                                             (amp_mask_hbm, amp_mask)))]
    for load in loads:
        load.start()
    barrier = pltpu.get_barrier_semaphore()

    def hi_peer(step):
        return ((hi + step) % n_hi) * CORES + core

    def greet(pair, virt):
        pl.semaphore_signal(barrier, inc=1, device_id=(pair, virt), device_id_type=MESH)

    greet(me_p, line * 2 + (1 - side))
    pl.when(line > 0)(lambda: greet(me_p, me_v - 2))
    pl.when(line < n_line - 1)(lambda: greet(me_p, me_v + 2))
    for step in range(1, n_hi):
        greet(hi_peer(step), me_v)
    greet(partner, me_v)

    tiles = int_mask.shape[1]
    repeat = spread(tiles, columns, 1)
    loads[0].wait()
    mask = jnp.broadcast_to(int_mask[...].astype(F32), (8, tiles)).astype(BF16)
    wide = jnp.dot(mask, repeat, preferred_element_type=F32)[:1].astype(BF16)
    loads[1].wait()
    for c in range(chunks):
        at = slice(c * CHUNK, (c + 1) * CHUNK)
        masked[c] = own[:, at] * wide[:, at]
    loads[2].wait()

    below, above = (line + n_line - 1) // n_line, (2 * n_line - 2 - line) // n_line
    pl.semaphore_wait(barrier, n_hi + 1 + below + above)

    def rows_of(pair):
        return pl.ds(pl.multiple_of(pair * depth, depth), depth)

    my_panel = panel.at[:, rows_of(me_p)]

    def to_hi(step, c):
        return pltpu.make_async_remote_copy(
            src_ref=masked.at[c], dst_ref=landed.at[step - 1, c],
            send_sem=x_send.at[step, c], recv_sem=x_recv.at[step, c],
            device_id=(hi_peer(step), me_v), device_id_type=MESH)

    def pass_on(step, c):
        held, place = landed.at[step - 1, c], panel.at[c, rows_of(((hi - step + n_hi) % n_hi) * CORES + core)]
        return pltpu.make_async_remote_copy(
            src_ref=held, dst_ref=place, send_sem=f_send.at[step, c], recv_sem=f_recv.at[step, c],
            device_id=(partner, me_v), device_id_type=MESH), pltpu.make_async_copy(held, place, x_keep.at[step, c])

    to_partner = pltpu.make_async_remote_copy(
        src_ref=masked, dst_ref=my_panel, send_sem=f_send.at[0, 0], recv_sem=f_recv.at[0, 0],
        device_id=(partner, me_v), device_id_type=MESH)

    def to_virt(step):
        other_side = side if step < n_line else 1 - side
        peer = ((line + step % n_line) % n_line) * 2 + other_side
        return pltpu.make_async_remote_copy(
            src_ref=own_amp, dst_ref=my_amps, send_sem=a_send.at[step], recv_sem=a_recv.at[step],
            device_id=(me_p, peer), device_id_type=MESH)

    def tell(token, step, virt):
        pl.semaphore_signal(token.at[step], inc=1, device_id=(me_p, virt), device_id_type=MESH)

    def tell_up(step):
        tell(up_token, step, me_v + 2)

    def tell_down(step):
        tell(down_token, step, me_v - 2)

    def reach(step):
        def below_side():
            pl.semaphore_wait(up_token.at[step], 1)
            if step + 1 < n_line:
                pl.when(line < n_line - 1)(lambda: tell_up(step + 1))
            to_virt(n_line - step).start()
            to_virt(2 * n_line - step).start()

        def above_side():
            pl.semaphore_wait(down_token.at[step], 1)
            if step + 1 < n_line:
                pl.when(line > 0)(lambda: tell_down(step + 1))
            to_virt(step).start()
            to_virt(n_line + step).start()

        pl.when(line - step >= 0)(below_side)
        pl.when(line + step < n_line)(above_side)

    keep = pltpu.make_async_copy(masked, my_panel, keep_sem.at[0])
    amps_keep = pltpu.make_async_copy(own_amp, my_amps, keep_sem.at[1])
    wide_keep = pltpu.make_async_copy(wide_mask, wide_out, keep_sem.at[2])
    pl.when(line < n_line - 1)(lambda: tell_up(1))
    pl.when(line > 0)(lambda: tell_down(1))
    for step in range(1, n_hi):
        to_hi(step, 0).start()
    to_virt(n_line).start()
    for c in range(1, chunks):
        for step in range(1, n_hi):
            to_hi(step, c).start()
    to_partner.start()
    keep.start()
    amps_keep.start()
    for step in range(1, n_line):
        reach(step)

    row_tiles, col_tiles = amp_mask.shape
    all_rows, depths = amps.shape
    loads[3].wait()
    tall = jnp.dot(spread(row_tiles, all_rows, 0), amp_mask[...].astype(F32).astype(BF16),
                   preferred_element_type=F32).astype(BF16)
    wide_mask[...] = jnp.dot(tall, spread(col_tiles, depths, 1), preferred_element_type=F32).astype(BF16)
    wide_keep.start()

    for c in range(chunks):
        for step in range(1, n_hi):
            to_hi(step, c).wait_recv()
            for copy in pass_on(step, c):
                copy.start()
    for step in range(1, n_virt):
        to_virt(step).wait()

    keep.wait()
    to_partner.wait()
    amps_keep.wait()
    wide_keep.wait()
    for c in range(chunks):
        for step in range(1, n_hi):
            to_hi(step, c).wait_send()
            for copy in pass_on(step, c):
                copy.wait()


def multiply(panel_hbm, amps_hbm, wide_hbm, out, panel, amps, wide_mask, result, load_sem, panel_sem, out_sem):
    chunks = panel.shape[0]
    all_rows = amps.shape[0]
    part = min(all_rows, 256)
    loads = [pltpu.make_async_copy(amps_hbm, amps, load_sem.at[0]),
             pltpu.make_async_copy(wide_hbm, wide_mask, load_sem.at[1])]
    blocks = [pltpu.make_async_copy(panel_hbm.at[c], panel.at[c], panel_sem.at[c]) for c in range(chunks)]
    stores = [pltpu.make_async_copy(result.at[c], out.at[:, pl.ds(c * CHUNK, CHUNK)], out_sem.at[c])
              for c in range(chunks)]
    for copy in loads + blocks:
        copy.start()
    for load in loads:
        load.wait()
    amps[...] = amps[...] * wide_mask[...]

    for c in range(chunks):
        blocks[c].wait()

        def some_rows(r, carry):
            at = pl.ds(r * part, part)
            result[c, at, :] = jnp.dot(amps[at, :], panel[c], preferred_element_type=F32).astype(BF16)
            return carry

        if all_rows == part:
            some_rows(0, 0)
        else:
            lax.fori_loop(0, all_rows // part, some_rows, 0)
        stores[c].start()
    for store in stores:
        store.wait()


def solution(mesh):
    n_pair, n_virt = mesh.shape["pair"], mesh.shape["virt"]
    n_hi = n_pair // CORES

    def on_device(amplitudes, integrals, amp_mask, integral_mask):
        rows, depths = amplitudes.shape
        depth, columns = integrals.shape
        all_rows = rows * n_virt
        chunks = columns // CHUNK
        dma = pltpu.SemaphoreType.DMA
        hbm = pl.BlockSpec(memory_space=pltpu.HBM)
        whole_panel = jax.ShapeDtypeStruct((chunks, depths, CHUNK), BF16)
        whole_amps = jax.ShapeDtypeStruct((all_rows, depths), BF16)
        panel, amps, wide_mask = pl.pallas_call(
            functools.partial(gather, n_pair, n_virt),
            out_shape=(whole_panel, whole_amps, whole_amps),
            in_specs=[hbm] * 4,
            out_specs=(hbm, hbm, hbm),
            scratch_shapes=[
                pltpu.VMEM((depth, columns), BF16),
                pltpu.VMEM((rows, depths), BF16),
                pltpu.VMEM((chunks, depth, CHUNK), BF16),
                pltpu.VMEM((max(n_hi - 1, 1), chunks, depth, CHUNK), BF16),
                pltpu.VMEM(amp_mask.shape, jnp.int32),
                pltpu.VMEM(integral_mask.shape, jnp.int32),
                pltpu.VMEM(whole_amps.shape, BF16),
                dma((4,)), dma((3,)),
                dma((n_hi, chunks)), dma((n_hi, chunks)), dma((n_hi, chunks)),
                dma((n_hi, chunks)), dma((n_hi, chunks)),
                dma((n_virt,)), dma((n_virt,)),
                pltpu.SemaphoreType.REGULAR((n_virt // 2,)), pltpu.SemaphoreType.REGULAR((n_virt // 2,)),
            ],
            compiler_params=pltpu.CompilerParams(
                collective_id=0, has_side_effects=True, vmem_limit_bytes=60 * 2 ** 20),
        )(amplitudes, integrals, amp_mask, integral_mask)
        return pl.pallas_call(
            multiply,
            out_shape=jax.ShapeDtypeStruct((all_rows, columns), BF16),
            in_specs=[hbm] * 3,
            out_specs=hbm,
            scratch_shapes=[
                pltpu.VMEM(whole_panel.shape, BF16),
                pltpu.VMEM(whole_amps.shape, BF16),
                pltpu.VMEM(whole_amps.shape, BF16),
                pltpu.VMEM((chunks, all_rows, CHUNK), BF16),
                dma((2,)), dma((chunks,)), dma((chunks,)),
            ],
            compiler_params=pltpu.CompilerParams(vmem_limit_bytes=60 * 2 ** 20),
        )(panel, amps, wide_mask)

    in_specs = (P(("pair", "virt"), None), P("pair", "virt"), P("pair", None), P("pair", "virt"))
    return jax.shard_map(
        on_device, mesh=mesh, in_specs=in_specs, out_specs=P("pair", "virt"), check_vma=False
    )
```

```python
import functools

import jax
import jax.numpy as jnp
from jax import lax
from jax.experimental import pallas as pl
from jax.experimental.pallas import tpu as pltpu
from jax.sharding import PartitionSpec as P

MESH = pl.DeviceIdType.MESH
CHUNK = 1024
CORES = 2
F32 = jnp.float32
BF16 = jnp.bfloat16


def spread(tiles, length, axis):
    shape = (length, tiles) if axis == 0 else (tiles, length)
    place = lax.broadcasted_iota(jnp.int32, shape, axis)
    tile = lax.broadcasted_iota(jnp.int32, shape, 1 - axis)
    size = length // tiles
    inside = (place >= tile * size) & (place < (tile + 1) * size)
    return jnp.where(inside, 1.0, 0.0).astype(BF16)


def gather(n_pair, n_virt, amp_hbm, int_hbm, amp_mask_hbm, int_mask_hbm, panel, amps, wide_out,
           own, own_amp, masked, landed, amp_mask, int_mask, wide_mask, load_sem, keep_sem, x_send, x_recv, x_keep,
           f_send, f_recv, a_send, a_recv, up_token, down_token):
    me_p, me_v = lax.axis_index("pair"), lax.axis_index("virt")
    n_hi = n_pair // CORES
    hi, core = me_p // CORES, me_p % CORES
    partner = hi * CORES + (1 - core)
    depth, columns = int_hbm.shape
    rows = amp_hbm.shape[0]
    chunks = panel.shape[0]

    line, side = me_v // 2, me_v % 2
    n_line = n_virt // 2
    my_amps = amps.at[pl.ds(pl.multiple_of(me_v * rows, rows), rows)]
    loads = [pltpu.make_async_copy(src, dst, load_sem.at[i])
             for i, (src, dst) in enumerate(((int_mask_hbm, int_mask), (int_hbm, own), (amp_hbm, own_amp),
                                             (amp_mask_hbm, amp_mask)))]
    for load in loads[:2]:
        load.start()
    barrier = pltpu.get_barrier_semaphore()

    def hi_peer(step):
        return ((hi + step) % n_hi) * CORES + core

    def greet(pair, virt):
        pl.semaphore_signal(barrier, inc=1, device_id=(pair, virt), device_id_type=MESH)

    greet(me_p, line * 2 + (1 - side))
    pl.when(line > 0)(lambda: greet(me_p, me_v - 2))
    pl.when(line < n_line - 1)(lambda: greet(me_p, me_v + 2))
    for step in range(1, n_hi):
        greet(hi_peer(step), me_v)
    greet(partner, me_v)
    for load in loads[2:]:
        load.start()

    tiles = int_mask.shape[1]
    repeat = spread(tiles, columns, 1)
    loads[0].wait()
    mask = jnp.broadcast_to(int_mask[...].astype(F32), (8, tiles)).astype(BF16)
    wide = jnp.dot(mask, repeat, preferred_element_type=F32)[:1].astype(BF16)
    loads[1].wait()

    def fill(c):
        at = slice(c * CHUNK, (c + 1) * CHUNK)
        masked[c] = own[:, at] * wide[:, at]

    fill(0)
    below, above = (line + n_line - 1) // n_line, (2 * n_line - 2 - line) // n_line
    pl.semaphore_wait(barrier, n_hi + 1 + below + above)

    def rows_of(pair):
        return pl.ds(pl.multiple_of(pair * depth, depth), depth)

    my_panel = panel.at[:, rows_of(me_p)]

    def to_hi(step, c):
        return pltpu.make_async_remote_copy(
            src_ref=masked.at[c], dst_ref=landed.at[step - 1, c],
            send_sem=x_send.at[step, c], recv_sem=x_recv.at[step, c],
            device_id=(hi_peer(step), me_v), device_id_type=MESH)

    def pass_on(step, c):
        held, place = landed.at[step - 1, c], panel.at[c, rows_of(((hi - step + n_hi) % n_hi) * CORES + core)]
        return pltpu.make_async_remote_copy(
            src_ref=held, dst_ref=place, send_sem=f_send.at[step, c], recv_sem=f_recv.at[step, c],
            device_id=(partner, me_v), device_id_type=MESH), pltpu.make_async_copy(held, place, x_keep.at[step, c])

    to_partner = pltpu.make_async_remote_copy(
        src_ref=masked, dst_ref=my_panel, send_sem=f_send.at[0, 0], recv_sem=f_recv.at[0, 0],
        device_id=(partner, me_v), device_id_type=MESH)

    def to_virt(step):
        other_side = side if step < n_line else 1 - side
        peer = ((line + step % n_line) % n_line) * 2 + other_side
        return pltpu.make_async_remote_copy(
            src_ref=own_amp, dst_ref=my_amps, send_sem=a_send.at[step], recv_sem=a_recv.at[step],
            device_id=(me_p, peer), device_id_type=MESH)

    def tell(token, step, virt):
        pl.semaphore_signal(token.at[step], inc=1, device_id=(me_p, virt), device_id_type=MESH)

    def tell_up(step):
        tell(up_token, step, me_v + 2)

    def tell_down(step):
        tell(down_token, step, me_v - 2)

    def reach(step):
        def below_side():
            pl.semaphore_wait(up_token.at[step], 1)
            if step + 1 < n_line:
                pl.when(line < n_line - 1)(lambda: tell_up(step + 1))
            to_virt(n_line - step).start()
            to_virt(2 * n_line - step).start()

        def above_side():
            pl.semaphore_wait(down_token.at[step], 1)
            if step + 1 < n_line:
                pl.when(line > 0)(lambda: tell_down(step + 1))
            to_virt(step).start()
            to_virt(n_line + step).start()

        pl.when(line - step >= 0)(below_side)
        pl.when(line + step < n_line)(above_side)

    keep = pltpu.make_async_copy(masked, my_panel, keep_sem.at[0])
    amps_keep = pltpu.make_async_copy(own_amp, my_amps, keep_sem.at[1])
    wide_keep = pltpu.make_async_copy(wide_mask, wide_out, keep_sem.at[2])
    for c in range(chunks):
        if c:
            fill(c)
        for step in range(1, n_hi):
            to_hi(step, c).start()
    pl.when(line < n_line - 1)(lambda: tell_up(1))
    pl.when(line > 0)(lambda: tell_down(1))
    loads[2].wait()
    to_virt(n_line).start()
    to_partner.start()
    keep.start()
    amps_keep.start()
    row_tiles, col_tiles = amp_mask.shape
    all_rows, depths = amps.shape
    loads[3].wait()
    tall = jnp.dot(spread(row_tiles, all_rows, 0), amp_mask[...].astype(F32).astype(BF16),
                   preferred_element_type=F32).astype(BF16)
    wide_mask[...] = jnp.dot(tall, spread(col_tiles, depths, 1), preferred_element_type=F32).astype(BF16)
    wide_keep.start()
    for step in range(1, n_line):
        reach(step)

    for c in range(chunks):
        for step in range(1, n_hi):
            to_hi(step, c).wait_recv()
            for copy in pass_on(step, c):
                copy.start()
    for step in range(1, n_virt):
        to_virt(step).wait()

    keep.wait()
    to_partner.wait()
    amps_keep.wait()
    wide_keep.wait()
    for c in range(chunks):
        for step in range(1, n_hi):
            to_hi(step, c).wait_send()
            for copy in pass_on(step, c):
                copy.wait()


def multiply(panel_hbm, amps_hbm, wide_hbm, out, panel, amps, wide_mask, result, load_sem, panel_sem, out_sem):
    chunks = panel.shape[0]
    all_rows = amps.shape[0]
    part = min(all_rows, 256)
    loads = [pltpu.make_async_copy(amps_hbm, amps, load_sem.at[0]),
             pltpu.make_async_copy(wide_hbm, wide_mask, load_sem.at[1])]
    blocks = [pltpu.make_async_copy(panel_hbm.at[c], panel.at[c], panel_sem.at[c]) for c in range(chunks)]
    stores = [pltpu.make_async_copy(result.at[c], out.at[:, pl.ds(c * CHUNK, CHUNK)], out_sem.at[c])
              for c in range(chunks)]
    for copy in loads + blocks:
        copy.start()
    for load in loads:
        load.wait()
    amps[...] = amps[...] * wide_mask[...]

    for c in range(chunks):
        blocks[c].wait()

        def some_rows(r, carry):
            at = pl.ds(r * part, part)
            result[c, at, :] = jnp.dot(amps[at, :], panel[c], preferred_element_type=F32).astype(BF16)
            return carry

        if all_rows == part:
            some_rows(0, 0)
        else:
            lax.fori_loop(0, all_rows // part, some_rows, 0)
        stores[c].start()
    for store in stores:
        store.wait()


def solution(mesh):
    n_pair, n_virt = mesh.shape["pair"], mesh.shape["virt"]
    n_hi = n_pair // CORES

    def on_device(amplitudes, integrals, amp_mask, integral_mask):
        rows, depths = amplitudes.shape
        depth, columns = integrals.shape
        all_rows = rows * n_virt
        chunks = columns // CHUNK
        dma = pltpu.SemaphoreType.DMA
        hbm = pl.BlockSpec(memory_space=pltpu.HBM)
        whole_panel = jax.ShapeDtypeStruct((chunks, depths, CHUNK), BF16)
        whole_amps = jax.ShapeDtypeStruct((all_rows, depths), BF16)
        panel, amps, wide_mask = pl.pallas_call(
            functools.partial(gather, n_pair, n_virt),
            out_shape=(whole_panel, whole_amps, whole_amps),
            in_specs=[hbm] * 4,
            out_specs=(hbm, hbm, hbm),
            scratch_shapes=[
                pltpu.VMEM((depth, columns), BF16),
                pltpu.VMEM((rows, depths), BF16),
                pltpu.VMEM((chunks, depth, CHUNK), BF16),
                pltpu.VMEM((max(n_hi - 1, 1), chunks, depth, CHUNK), BF16),
                pltpu.VMEM(amp_mask.shape, jnp.int32),
                pltpu.VMEM(integral_mask.shape, jnp.int32),
                pltpu.VMEM(whole_amps.shape, BF16),
                dma((4,)), dma((3,)),
                dma((n_hi, chunks)), dma((n_hi, chunks)), dma((n_hi, chunks)),
                dma((n_hi, chunks)), dma((n_hi, chunks)),
                dma((n_virt,)), dma((n_virt,)),
                pltpu.SemaphoreType.REGULAR((n_virt // 2,)), pltpu.SemaphoreType.REGULAR((n_virt // 2,)),
            ],
            compiler_params=pltpu.CompilerParams(
                collective_id=0, has_side_effects=True, vmem_limit_bytes=60 * 2 ** 20),
        )(amplitudes, integrals, amp_mask, integral_mask)
        return pl.pallas_call(
            multiply,
            out_shape=jax.ShapeDtypeStruct((all_rows, columns), BF16),
            in_specs=[hbm] * 3,
            out_specs=hbm,
            scratch_shapes=[
                pltpu.VMEM(whole_panel.shape, BF16),
                pltpu.VMEM(whole_amps.shape, BF16),
                pltpu.VMEM(whole_amps.shape, BF16),
                pltpu.VMEM((chunks, all_rows, CHUNK), BF16),
                dma((2,)), dma((chunks,)), dma((chunks,)),
            ],
            compiler_params=pltpu.CompilerParams(vmem_limit_bytes=60 * 2 ** 20),
        )(panel, amps, wide_mask)

    in_specs = (P(("pair", "virt"), None), P("pair", "virt"), P("pair", None), P("pair", "virt"))
    return jax.shard_map(
        on_device, mesh=mesh, in_specs=in_specs, out_specs=P("pair", "virt"), check_vma=False
    )
```

```python
import functools

import jax
import jax.numpy as jnp
from jax import lax
from jax.experimental import pallas as pl
from jax.experimental.pallas import tpu as pltpu
from jax.sharding import PartitionSpec as P

MESH = pl.DeviceIdType.MESH
CHUNK = 1024
CORES = 2
F32 = jnp.float32
BF16 = jnp.bfloat16


def spread(tiles, length, axis):
    shape = (length, tiles) if axis == 0 else (tiles, length)
    place = lax.broadcasted_iota(jnp.int32, shape, axis)
    tile = lax.broadcasted_iota(jnp.int32, shape, 1 - axis)
    size = length // tiles
    inside = (place >= tile * size) & (place < (tile + 1) * size)
    return jnp.where(inside, 1.0, 0.0).astype(BF16)


def gather(n_pair, n_virt, amp_hbm, int_hbm, amp_mask_hbm, int_mask_hbm, panel, amps, wide_out,
           own, own_amp, masked, landed, amp_mask, int_mask, wide_mask, load_sem, keep_sem, x_send, x_recv, x_keep,
           f_send, f_recv, a_send, a_recv, up_token, down_token):
    me_p, me_v = lax.axis_index("pair"), lax.axis_index("virt")
    n_hi = n_pair // CORES
    hi, core = me_p // CORES, me_p % CORES
    partner = hi * CORES + (1 - core)
    depth, columns = int_hbm.shape
    rows = amp_hbm.shape[0]
    chunks = panel.shape[0]

    line, side = me_v // 2, me_v % 2
    n_line = n_virt // 2
    my_amps = amps.at[pl.ds(pl.multiple_of(me_v * rows, rows), rows)]
    loads = [pltpu.make_async_copy(src, dst, load_sem.at[i])
             for i, (src, dst) in enumerate(((int_mask_hbm, int_mask), (int_hbm, own), (amp_hbm, own_amp),
                                             (amp_mask_hbm, amp_mask)))]
    for load in loads[:2]:
        load.start()
    barrier = pltpu.get_barrier_semaphore()

    def hi_peer(step):
        return ((hi + step) % n_hi) * CORES + core

    def greet(pair, virt):
        pl.semaphore_signal(barrier, inc=1, device_id=(pair, virt), device_id_type=MESH)

    greet(me_p, line * 2 + (1 - side))
    pl.when(line > 0)(lambda: greet(me_p, me_v - 2))
    pl.when(line < n_line - 1)(lambda: greet(me_p, me_v + 2))
    for step in range(1, n_hi):
        greet(hi_peer(step), me_v)
    greet(partner, me_v)
    for load in loads[2:]:
        load.start()

    tiles = int_mask.shape[1]
    repeat = spread(tiles, columns, 1)
    loads[0].wait()
    mask = jnp.broadcast_to(int_mask[...].astype(F32), (8, tiles)).astype(BF16)
    wide = jnp.dot(mask, repeat, preferred_element_type=F32)[:1].astype(BF16)
    loads[1].wait()

    def fill(c):
        at = slice(c * CHUNK, (c + 1) * CHUNK)
        masked[c] = own[:, at] * wide[:, at]

    fill(0)
    below, above = (line + n_line - 1) // n_line, (2 * n_line - 2 - line) // n_line
    pl.semaphore_wait(barrier, n_hi + 1 + below + above)

    def rows_of(pair):
        return pl.ds(pl.multiple_of(pair * depth, depth), depth)

    my_panel = panel.at[:, rows_of(me_p)]

    def half(c):
        return pl.ds((c % 2) * (depth // 2), depth // 2)

    def to_hi(step, c):
        return pltpu.make_async_remote_copy(
            src_ref=masked.at[c // 2, half(c)], dst_ref=landed.at[step - 1, c // 2, half(c)],
            send_sem=x_send.at[step, c], recv_sem=x_recv.at[step, c],
            device_id=(hi_peer(step), me_v), device_id_type=MESH)

    def pass_on(step, c):
        first = (((hi - step + n_hi) % n_hi) * CORES + core) * depth + (c % 2) * (depth // 2)
        held = landed.at[step - 1, c // 2, half(c)]
        place = panel.at[c // 2, pl.ds(pl.multiple_of(first, depth // 2), depth // 2)]
        return pltpu.make_async_remote_copy(
            src_ref=held, dst_ref=place, send_sem=f_send.at[step, c], recv_sem=f_recv.at[step, c],
            device_id=(partner, me_v), device_id_type=MESH), pltpu.make_async_copy(held, place, x_keep.at[step, c])

    to_partner = pltpu.make_async_remote_copy(
        src_ref=masked, dst_ref=my_panel, send_sem=f_send.at[0, 0], recv_sem=f_recv.at[0, 0],
        device_id=(partner, me_v), device_id_type=MESH)

    def to_virt(step):
        other_side = side if step < n_line else 1 - side
        peer = ((line + step % n_line) % n_line) * 2 + other_side
        return pltpu.make_async_remote_copy(
            src_ref=own_amp, dst_ref=my_amps, send_sem=a_send.at[step], recv_sem=a_recv.at[step],
            device_id=(me_p, peer), device_id_type=MESH)

    def tell(token, step, virt):
        pl.semaphore_signal(token.at[step], inc=1, device_id=(me_p, virt), device_id_type=MESH)

    def tell_up(step):
        tell(up_token, step, me_v + 2)

    def tell_down(step):
        tell(down_token, step, me_v - 2)

    def reach(step):
        def below_side():
            pl.semaphore_wait(up_token.at[step], 1)
            if step + 1 < n_line:
                pl.when(line < n_line - 1)(lambda: tell_up(step + 1))
            to_virt(n_line - step).start()
            to_virt(2 * n_line - step).start()

        def above_side():
            pl.semaphore_wait(down_token.at[step], 1)
            if step + 1 < n_line:
                pl.when(line > 0)(lambda: tell_down(step + 1))
            to_virt(step).start()
            to_virt(n_line + step).start()

        pl.when(line - step >= 0)(below_side)
        pl.when(line + step < n_line)(above_side)

    keep = pltpu.make_async_copy(masked, my_panel, keep_sem.at[0])
    amps_keep = pltpu.make_async_copy(own_amp, my_amps, keep_sem.at[1])
    wide_keep = pltpu.make_async_copy(wide_mask, wide_out, keep_sem.at[2])
    for c in range(2 * chunks):
        if c and c % 2 == 0:
            fill(c // 2)
        for step in range(1, n_hi):
            to_hi(step, c).start()
    pl.when(line < n_line - 1)(lambda: tell_up(1))
    pl.when(line > 0)(lambda: tell_down(1))
    loads[2].wait()
    to_virt(n_line).start()
    to_partner.start()
    keep.start()
    amps_keep.start()
    row_tiles, col_tiles = amp_mask.shape
    all_rows, depths = amps.shape
    loads[3].wait()
    tall = jnp.dot(spread(row_tiles, all_rows, 0), amp_mask[...].astype(F32).astype(BF16),
                   preferred_element_type=F32).astype(BF16)
    wide_mask[...] = jnp.dot(tall, spread(col_tiles, depths, 1), preferred_element_type=F32).astype(BF16)
    wide_keep.start()
    for step in range(1, n_line):
        reach(step)

    for c in range(2 * chunks):
        for step in range(1, n_hi):
            to_hi(step, c).wait_recv()
            for copy in pass_on(step, c):
                copy.start()
    for step in range(1, n_virt):
        to_virt(step).wait()

    keep.wait()
    to_partner.wait()
    amps_keep.wait()
    wide_keep.wait()
    for c in range(2 * chunks):
        for step in range(1, n_hi):
            to_hi(step, c).wait_send()
            for copy in pass_on(step, c):
                copy.wait()


def multiply(panel_hbm, amps_hbm, wide_hbm, out, panel, amps, wide_mask, result, load_sem, panel_sem, out_sem):
    chunks = panel.shape[0]
    all_rows = amps.shape[0]
    part = min(all_rows, 256)
    loads = [pltpu.make_async_copy(amps_hbm, amps, load_sem.at[0]),
             pltpu.make_async_copy(wide_hbm, wide_mask, load_sem.at[1])]
    blocks = [pltpu.make_async_copy(panel_hbm.at[c], panel.at[c], panel_sem.at[c]) for c in range(chunks)]
    stores = [pltpu.make_async_copy(result.at[c], out.at[:, pl.ds(c * CHUNK, CHUNK)], out_sem.at[c])
              for c in range(chunks)]
    for copy in loads + blocks:
        copy.start()
    for load in loads:
        load.wait()
    amps[...] = amps[...] * wide_mask[...]

    for c in range(chunks):
        blocks[c].wait()

        def some_rows(r, carry):
            at = pl.ds(r * part, part)
            result[c, at, :] = jnp.dot(amps[at, :], panel[c], preferred_element_type=F32).astype(BF16)
            return carry

        if all_rows == part:
            some_rows(0, 0)
        else:
            lax.fori_loop(0, all_rows // part, some_rows, 0)
        stores[c].start()
    for store in stores:
        store.wait()


def solution(mesh):
    n_pair, n_virt = mesh.shape["pair"], mesh.shape["virt"]
    n_hi = n_pair // CORES

    def on_device(amplitudes, integrals, amp_mask, integral_mask):
        rows, depths = amplitudes.shape
        depth, columns = integrals.shape
        all_rows = rows * n_virt
        chunks = columns // CHUNK
        dma = pltpu.SemaphoreType.DMA
        hbm = pl.BlockSpec(memory_space=pltpu.HBM)
        whole_panel = jax.ShapeDtypeStruct((chunks, depths, CHUNK), BF16)
        whole_amps = jax.ShapeDtypeStruct((all_rows, depths), BF16)
        panel, amps, wide_mask = pl.pallas_call(
            functools.partial(gather, n_pair, n_virt),
            out_shape=(whole_panel, whole_amps, whole_amps),
            in_specs=[hbm] * 4,
            out_specs=(hbm, hbm, hbm),
            scratch_shapes=[
                pltpu.VMEM((depth, columns), BF16),
                pltpu.VMEM((rows, depths), BF16),
                pltpu.VMEM((chunks, depth, CHUNK), BF16),
                pltpu.VMEM((max(n_hi - 1, 1), chunks, depth, CHUNK), BF16),
                pltpu.VMEM(amp_mask.shape, jnp.int32),
                pltpu.VMEM(integral_mask.shape, jnp.int32),
                pltpu.VMEM(whole_amps.shape, BF16),
                dma((4,)), dma((3,)),
                dma((n_hi, 2 * chunks)), dma((n_hi, 2 * chunks)), dma((n_hi, 2 * chunks)),
                dma((n_hi, 2 * chunks)), dma((n_hi, 2 * chunks)),
                dma((n_virt,)), dma((n_virt,)),
                pltpu.SemaphoreType.REGULAR((n_virt // 2,)), pltpu.SemaphoreType.REGULAR((n_virt // 2,)),
            ],
            compiler_params=pltpu.CompilerParams(
                collective_id=0, has_side_effects=True, vmem_limit_bytes=60 * 2 ** 20),
        )(amplitudes, integrals, amp_mask, integral_mask)
        return pl.pallas_call(
            multiply,
            out_shape=jax.ShapeDtypeStruct((all_rows, columns), BF16),
            in_specs=[hbm] * 3,
            out_specs=hbm,
            scratch_shapes=[
                pltpu.VMEM(whole_panel.shape, BF16),
                pltpu.VMEM(whole_amps.shape, BF16),
                pltpu.VMEM(whole_amps.shape, BF16),
                pltpu.VMEM((chunks, all_rows, CHUNK), BF16),
                dma((2,)), dma((chunks,)), dma((chunks,)),
            ],
            compiler_params=pltpu.CompilerParams(vmem_limit_bytes=60 * 2 ** 20),
        )(panel, amps, wide_mask)

    in_specs = (P(("pair", "virt"), None), P("pair", "virt"), P("pair", None), P("pair", "virt"))
    return jax.shard_map(
        on_device, mesh=mesh, in_specs=in_specs, out_specs=P("pair", "virt"), check_vma=False
    )
```
